32 devices in a mesh: clips: 2 (over y), ha: 4 (over z), wa: 2 (over core), ta: 2 (over x).
Axes of the slice: x: 2, y: 2, z: 4, core: 2. Of those that a mesh axis runs over, the one named last changes fastest.
Arguments:
- frames: bfloat16 [8, 16, 256, 128], P(('clips', 'ta'), 'ha', 'wa'), parts along dimension 0, may hold values from -12 to 12
- past_first: bfloat16 [4, 16, 256, 128], P('clips', 'ha', 'wa'), parts along dimension 0, may hold values from -6 to 6
- past_second: bfloat16 [4, 16, 256, 128], P('clips', 'ha', 'wa'), parts along dimension 0, may hold values from -6 to 6
- gain_first: float32 [128], replicated, may hold values from 0.5 to 1.5
- shift_first: float32 [128], replicated, may hold values from -3 to 3
- kernel_first: bfloat16 [3, 3, 3, 128, 128], replicated, may hold values from -0.109375 to 0.109375
- bias_first: float32 [128], replicated, may hold values from -2 to 2
- gain_second: float32 [128], replicated, may hold values from 0.5 to 1.5
- shift_second: float32 [128], replicated, may hold values from -3 to 3
- kernel_second: bfloat16 [3, 3, 3, 128, 128], replicated, may hold values from -0.109375 to 0.109375
- bias_second: float32 [128], replicated, may hold values from -2 to 2
Outputs:
- decoded: bfloat16 [8, 16, 256, 128], P(('clips', 'ta'), 'ha', 'wa'), parts along dimension 0
The draws below stay inside these ranges and needn't reach their ends.
There are 2 independent parts, one for each index of `clips`. The reference program is written for one: setup_inputs(seed, part) draws one part's arguments, and reference() takes and returns one part's arrays. A program takes and returns all parts, laid end to end along the dimension named above; an argument that names none is the same for every part. Nothing has to cross between parts.
All inputs are finite; a program needn't handle non-finite values.
Results may differ from the reference program's by a relative error of at most 0.0039.
Values may be sent and summed in bfloat16 or wider, within the bound.
A program may use at most 64 MiB of HBM per device.

```python
import jax
import jax.numpy as jnp
from jax import lax

C = 128
G = 32
HB = 4
WB = 128
FRAMES = 4
H = 16
W = 256


def draw_frames(key, part):
    base = jax.random.fold_in(key, 11)
    key_noise = jax.random.fold_in(base, 0)
    key_rough = jax.random.fold_in(base, 1)
    key_band = jax.random.fold_in(base, 3)
    key_frame = jax.random.fold_in(base, 4)
    key_chan = jax.random.fold_in(base, 5)
    ramp = (jnp.arange(H, dtype=jnp.float32) / max(H - 1, 1)).reshape(1, H, 1, 1)
    time_ramp = (jnp.arange(FRAMES, dtype=jnp.float32) / max(FRAMES - 1, 1)).reshape(FRAMES, 1, 1, 1)
    band_index = (jnp.arange(W, dtype=jnp.int32) // WB).astype(jnp.float32)
    band_step = (band_index / max(W // WB - 1, 1)).reshape(1, 1, W, 1)
    rough = jax.random.uniform(key_rough, (FRAMES, H, W, 1), jnp.float32, 0.0, 1.0)
    height_log = jax.random.uniform(key_band, (H // HB,), jnp.float32, -1.0, 1.0)
    height_log = jnp.repeat(height_log, HB, total_repeat_length=H).reshape(1, H, 1, 1)
    frame_log = jax.random.uniform(key_frame, (FRAMES, 1, 1, 1), jnp.float32, -1.0, 1.0)
    chan_scale = jnp.exp(jax.random.uniform(key_chan, (1, 1, 1, C), jnp.float32, -0.7, 0.7))
    scale = 10.0 ** (0.5 * ramp + 0.4 * time_ramp + 0.4 * band_step + 0.5 * rough - 1.5)
    scale = scale * jnp.exp(height_log + frame_log)
    noise = jax.random.normal(key_noise, (FRAMES, H, W, C), jnp.float32)
    values = noise * chan_scale * scale
    return jnp.clip(values, -12.0, 12.0).astype(jnp.bfloat16)


def block_levels(key, extent, pieces, smallest, largest):
    def one(axis_at, shards_of):
        draws = jax.random.uniform(jax.random.fold_in(jax.random.fold_in(key, 6), axis_at), (shards_of,), jnp.float32, smallest / len(pieces), largest / len(pieces))
        return jnp.repeat(jnp.exp(draws), extent[axis_at] // shards_of).reshape((-1,) + (1,) * (len(extent) - axis_at - 1))

    factor_of = one(*pieces[0])
    for cut in pieces[1:]:
        factor_of = factor_of * one(*cut)
    return factor_of


def bell_draw(rng, dims, spread, most, shards=(), kind=jnp.bfloat16):
    drawn = spread * jax.random.normal(rng, dims, jnp.float32)
    if shards:
        drawn = drawn * block_levels(rng, dims, shards, -0.22, 0.18)
    return jnp.clip(drawn, -most, most).astype(kind)


def setup_inputs(seed: int = 0, part: int = 0) -> dict:
    splits = jax.random.split(jax.random.key(seed), 12)
    part_keys = jax.random.split(jax.random.fold_in(splits[11], part), 12)
    frames = draw_frames(jax.random.fold_in(jax.random.fold_in(splits[11], part), 71), part)
    past_first = bell_draw(part_keys[1], (2, H, W, C), 1.0, 6.0, ((1, 4), (2, 2)))
    past_second = bell_draw(part_keys[2], (2, H, W, C), 1.0, 6.0, ((1, 4), (2, 2)))
    gain_first = jnp.clip(jax.random.uniform(splits[3], (C,), jnp.float32, 0.5, 1.5), 0.5, 1.5)
    shift_first = bell_draw(splits[4], (C,), 0.5, 3.0, (), jnp.float32)
    kernel_first = bell_draw(splits[5], (3, 3, 3, C, C), (27 * C) ** -0.5, 0.109375)
    bias_first = bell_draw(splits[6], (C,), 0.3, 2.0, (), jnp.float32)
    gain_second = jnp.clip(jax.random.uniform(splits[7], (C,), jnp.float32, 0.5, 1.5), 0.5, 1.5)
    shift_second = bell_draw(splits[8], (C,), 0.5, 3.0, (), jnp.float32)
    kernel_second = bell_draw(splits[9], (3, 3, 3, C, C), (27 * C) ** -0.5, 0.109375)
    bias_second = bell_draw(splits[10], (C,), 0.3, 2.0, (), jnp.float32)
    return {"frames": frames, "past_first": past_first, "past_second": past_second, "gain_first": gain_first, "shift_first": shift_first, "kernel_first": kernel_first, "bias_first": bias_first, "gain_second": gain_second, "shift_second": shift_second, "kernel_second": kernel_second, "bias_second": bias_second}


EPS = 1e-06

def norm_silu(value, gain, shift):
    nframe, rows, cols, chans = value.shape
    grouped = value.reshape(nframe, rows, cols, G, chans // G)
    mean = lax.optimization_barrier(jnp.mean(grouped, axis=(0, 1, 2, 4)))
    square = lax.optimization_barrier(jnp.mean(grouped * grouped, axis=(0, 1, 2, 4)))
    inverse = lax.rsqrt(square - mean * mean + EPS)
    mean_chan = jnp.repeat(mean, chans // G)
    inverse_chan = jnp.repeat(inverse, chans // G)
    return jax.nn.silu((value - mean_chan) * inverse_chan * gain + shift)

def causal_conv(past, current, kernel, bias):
    joined = jnp.concatenate([past, current], axis=0)
    padded = jnp.pad(joined, ((0, 0), (1, 1), (1, 1), (0, 0)))
    nframe = current.shape[0]
    rows = current.shape[1]
    cols = current.shape[2]
    chans = current.shape[3]
    stacked = kernel.reshape(3, 3, 3 * chans, chans)
    outputs = []
    for frame in range(nframe):
        total = jnp.zeros((rows * cols, chans), jnp.float32) + bias
        for time_step in range(3):
            for row_step in range(3):
                slab = jnp.concatenate([padded[frame + time_step, row_step:row_step + rows, col_step:col_step + cols, :] for col_step in range(3)], axis=-1)
                total = total + jnp.dot(slab.reshape(rows * cols, 3 * chans), stacked[time_step, row_step], preferred_element_type=jnp.float32)
        outputs.append(total.reshape(rows, cols, chans))
    return jnp.stack(outputs, axis=0)

def reference(frames, past_first, past_second, gain_first, shift_first, kernel_first, bias_first, gain_second, shift_second, kernel_second, bias_second):
    source = frames.astype(jnp.float32)
    act_one = norm_silu(source, gain_first, shift_first).astype(jnp.bfloat16)
    hidden = causal_conv(past_first, act_one, kernel_first, bias_first)
    act_two = norm_silu(hidden, gain_second, shift_second).astype(jnp.bfloat16)
    result = causal_conv(past_second, act_two, kernel_second, bias_second) + source
    return result.astype(jnp.bfloat16)
```

```python
import functools

import jax
import jax.numpy as jnp
from jax import lax
from jax.experimental import pallas as pl
from jax.experimental.pallas import tpu as pltpu
from jax.sharding import PartitionSpec as P

EPS = 1e-06
G = 32
PAD = 16
MESH = pl.DeviceIdType.MESH
DIRECTIONS = [(dh, dw) for dh in (-1, 0, 1) for dw in (-1, 0, 1) if (dh, dw) != (0, 0)]


def body(
    sizes,
    frames,
    past_first,
    past_second,
    gain_first,
    shift_first,
    kernel_first,
    bias_first,
    gain_second,
    shift_second,
    kernel_second,
    bias_second,
    out,
    raw,
    hid_edge,
    hid,
    line,
    cols_one,
    cols_two,
    weight_one,
    weight_two,
    stat_own,
    stat_in,
    local_sem,
    raw_send,
    raw_recv,
    hid_send,
    hid_recv,
    time_send,
    time_recv,
    stat_send,
    stat_recv,
):
    nha, nwa, nta = sizes
    peers = nha * nwa * nta
    _, nframe, rows2, width, chans = raw.shape
    rows, cols = rows2 - 2, width - 2 * PAD
    ha, wa, ta = lax.axis_index("ha"), lax.axis_index("wa"), lax.axis_index("ta")
    me = (ha * nwa + wa) * nta + ta
    count = float(nframe * rows * cols * (chans // G) * peers)

    def place(k):
        other = lax.rem(me + k, peers)
        return {
            "ha": other // (nwa * nta),
            "wa": lax.rem(other // nta, nwa),
            "ta": lax.rem(other, nta),
        }

    def inner(buf, slot):
        return buf.at[slot, :, pl.ds(1, rows), pl.ds(PAD, cols), :]

    load_frames = pltpu.make_async_copy(frames, inner(raw, 2), local_sem.at[0])
    load_past = pltpu.make_async_copy(past_first, inner(raw, jnp.maximum(1 - ta, 0)), local_sem.at[1])
    load_second = pltpu.make_async_copy(past_second, inner(hid_edge, 0), local_sem.at[2])
    load_w1 = pltpu.make_async_copy(kernel_first, weight_one, local_sem.at[3])
    load_w2 = pltpu.make_async_copy(kernel_second, weight_two, local_sem.at[4])

    def halo_copy(buf, slot, send, recv, d):
        dh, dw = DIRECTIONS[d]
        row_from, row_to, nrow = {-1: (1, rows + 1, 1), 0: (1, 1, rows), 1: (rows, 0, 1)}[dh]
        col_from, col_to, ncol = {
            -1: (PAD, PAD + cols, PAD),
            0: (PAD, PAD, cols),
            1: (cols, 0, PAD),
        }[dw]
        copy = pltpu.make_async_remote_copy(
            src_ref=buf.at[slot, :, pl.ds(row_from, nrow), pl.ds(col_from, ncol), :],
            dst_ref=buf.at[slot, :, pl.ds(row_to, nrow), pl.ds(col_to, ncol), :],
            send_sem=send.at[slot, d],
            recv_sem=recv.at[slot, d],
            device_id={"ha": ha + dh, "wa": wa + dw},
            device_id_type=MESH,
        )
        to_h, to_w = ha + dh, wa + dw
        from_h, from_w = ha - dh, wa - dw
        goes = (to_h >= 0) & (to_h < nha) & (to_w >= 0) & (to_w < nwa)
        comes = (from_h >= 0) & (from_h < nha) & (from_w >= 0) & (from_w < nwa)
        return copy, goes, comes

    def halo(action, buf, slot, send, recv, beside):
        for d in range(len(DIRECTIONS)):
            if (DIRECTIONS[d][0] == 0) not in beside:
                continue
            copy, goes, comes = halo_copy(buf, slot, send, recv, d)
            if action == "start":
                pl.when(goes)(copy.start)
            elif action == "recv":
                pl.when(comes)(copy.wait_recv)
            else:
                pl.when(goes)(copy.wait_send)

    def raw_halo(action, slot, beside=(False, True)):
        halo(action, raw, slot, raw_send, raw_recv, beside)

    def hid_halo(action, slot):
        halo(action, hid_edge, slot, hid_send, hid_recv, (False, True))

    def time_copies(step):
        slot = 2 - step
        parts = ((1, 1), (rows, 1), (2, rows - 2))
        return [
            pltpu.make_async_remote_copy(
                src_ref=raw.at[2, :, pl.ds(first, n), pl.ds(PAD, cols), :],
                dst_ref=raw.at[slot, :, pl.ds(first, n), pl.ds(PAD, cols), :],
                send_sem=time_send.at[step - 1, i],
                recv_sem=time_recv.at[step - 1, i],
                device_id={"ta": ta + step},
                device_id_type=MESH,
            )
            for i, (first, n) in enumerate(parts)
        ]

    steps = [step for step in (1, 2) if step < nta]

    def stat_copy(which, k):
        return pltpu.make_async_remote_copy(
            src_ref=stat_own.at[which],
            dst_ref=stat_in.at[which, k - 1],
            send_sem=stat_send.at[which],
            recv_sem=stat_recv.at[which],
            device_id=place(k),
            device_id_type=MESH,
        )

    def send_stats(which):
        @pl.loop(1, peers)
        def _(k):
            stat_copy(which, k).start()

    def group_total(which, sem):
        pltpu.make_async_copy(stat_in.at[which], stat_in.at[which], stat_recv.at[which]).wait()
        total = stat_own[which] + jnp.sum(stat_in[which], axis=0)
        lane = lax.broadcasted_iota(jnp.int32, total.shape, 1)
        for shift in (1, 2):
            low = lax.rem(lane, 2 * shift) < shift
            total = total + jnp.where(
                low, pltpu.roll(total, chans - shift, 1), pltpu.roll(total, shift, 1)
            )
        return total

    def scale_of(which, gain):
        total = group_total(which, stat_recv)
        mean = total[0:1] / count
        inverse = lax.rsqrt(total[1:2] / count - mean * mean + EPS)
        return mean, inverse * gain[...]

    def put_stats(which, first, second):
        stat_own[which, 0:1, :] = jnp.sum(first, axis=0, keepdims=True)
        stat_own[which, 1:2, :] = jnp.sum(second, axis=0, keepdims=True)

    def silu(v):
        half = 0.5 * v
        return half + half * jnp.tanh(half)

    def spread(dst, frame, row, value):
        low = jnp.where(wa > 0, 0, PAD)
        high = jnp.where(wa < nwa - 1, width, PAD + cols)
        live = ((row > 0) | (ha > 0)) & ((row < rows + 1) | (ha < nha - 1))
        high = jnp.where(live, high, 0)
        place_at = lax.broadcasted_iota(jnp.int32, (width, chans), 0)
        value = jnp.where((place_at >= low) & (place_at < high), value, 0.0)
        line[...] = value
        dst[frame, row, :, 0:chans] = line[pl.ds(PAD - 1, cols), :].astype(jnp.bfloat16)
        dst[frame, row, :, chans : 2 * chans] = value[PAD : PAD + cols].astype(jnp.bfloat16)
        dst[frame, row, :, 2 * chans :] = line[pl.ds(PAD + 1, cols), :].astype(jnp.bfloat16)

    def each_row(work):
        @pl.loop(0, nframe * rows2)
        def _(i):
            work(i // rows2, lax.rem(i, rows2))

    def spread_plain(dst, base, buf, slot):
        each_row(lambda f, r: spread(dst, base + f, r, buf[slot, f, r].astype(jnp.float32)))

    def spread_act(dst, base, slot, mean, scale, shift):
        def work(f, r):
            value = raw[slot, f, r].astype(jnp.float32)
            spread(dst, base + f, r, silu((value - mean) * scale + shift[...]))

        each_row(work)

    def spread_hidden(dst, base, slot, mean, scale, shift):
        def act(value):
            return silu((value - mean) * scale + shift[...])

        @pl.loop(0, nframe * rows)
        def _(i):
            f, r = i // rows, lax.rem(i, rows)
            edge = hid_edge[slot, f, r + 1].astype(jnp.float32)
            value = jnp.concatenate([edge[:PAD], hid[slot, f, r], edge[PAD + cols :]], axis=0)
            spread(dst, base + f, r + 1, act(value))

        @pl.loop(0, nframe * 2)
        def _(i):
            f, r = i // 2, lax.rem(i, 2) * (rows + 1)
            spread(dst, base + f, r, act(hid_edge[slot, f, r].astype(jnp.float32)))

    def conv_pair(src, base, weight, bias):
        def slab(f):
            return jnp.concatenate(
                [src[base + f, b : b + rows].reshape(rows * cols, 3 * chans) for b in range(3)],
                axis=1,
            )

        def dot(left, right):
            return jnp.dot(left, right, preferred_element_type=jnp.float32)

        both = dot(slab(1), jnp.concatenate([weight[1], weight[0]], axis=1))
        both = both + dot(slab(2), jnp.concatenate([weight[2], weight[1]], axis=1))
        one = both[:, :chans] + dot(slab(0), weight[0]) + bias[...]
        two = both[:, chans:] + dot(slab(3), weight[2]) + bias[...]
        return one, two

    def keep_hidden(slot, pair):
        for f, value in enumerate(pair):
            block = value.reshape(rows, cols, chans)
            hid[slot, f] = block
            hid_edge[slot, f, 1 : rows + 1, PAD : PAD + cols, :] = block.astype(jnp.bfloat16)

    load_frames.start()

    @pl.when(ta < 2)
    def _():
        load_past.start()

    @pl.when(ta == 0)
    def _():
        load_second.start()

    load_w1.start()
    load_w2.start()
    barrier = pltpu.get_barrier_semaphore()

    @pl.loop(1, peers)
    def _(k):
        pl.semaphore_signal(barrier, inc=1, device_id=place(k), device_id_type=MESH)

    load_frames.wait()
    first = jnp.zeros((cols, chans), jnp.float32)
    second = jnp.zeros((cols, chans), jnp.float32)
    for f in range(nframe):
        for r in range(rows):
            value = raw[2, f, 1 + r, PAD : PAD + cols, :].astype(jnp.float32)
            first = first + value
            second = second + value * value
    put_stats(0, first, second)
    pl.semaphore_wait(barrier, peers - 1)

    for step in steps:

        @pl.when(ta + step < nta)
        def _():
            for copy in time_copies(step):
                copy.start()

    send_stats(0)
    raw_halo("start", 2)

    @pl.when(ta == 0)
    def _():
        load_past.wait()
        raw_halo("start", 1)
        load_second.wait()
        hid_halo("start", 0)

    @pl.when(ta == 1)
    def _():
        load_past.wait()
        raw_halo("start", 0)

    mean_one, scale_one = scale_of(0, gain_first)
    raw_halo("recv", 2)
    spread_act(cols_one, 4, 2, mean_one, scale_one, shift_first)

    @pl.when(ta == 0)
    def _():
        raw_halo("recv", 1)
        spread_plain(cols_one, 2, raw, 1)
        hid_halo("recv", 0)
        spread_plain(cols_two, 0, hid_edge, 0)

    @pl.when(ta > 0)
    def _():
        def arrive(step):
            for copy in time_copies(step)[:2]:
                copy.wait_recv()
            raw_halo("start", 2 - step, (False,))

        arrive(1)

        @pl.when(ta == 1)
        def _():
            raw_halo("recv", 0)
            spread_plain(cols_one, 0, raw, 0)

        if nta > 2:

            @pl.when(ta > 1)
            def _():
                arrive(2)
                time_copies(2)[2].wait_recv()
                raw_halo("start", 0, (True,))
                raw_halo("recv", 0)
                spread_act(cols_one, 0, 0, mean_one, scale_one, shift_first)

        time_copies(1)[2].wait_recv()
        raw_halo("start", 1, (True,))
        raw_halo("recv", 1)
        spread_act(cols_one, 2, 1, mean_one, scale_one, shift_first)

    load_w1.wait()
    pair = conv_pair(cols_one, 2, weight_one, bias_first)
    put_stats(1, pair[0] + pair[1], pair[0] * pair[0] + pair[1] * pair[1])
    send_stats(1)
    keep_hidden(1, pair)
    hid_halo("start", 1)

    @pl.when(ta > 0)
    def _():
        keep_hidden(0, conv_pair(cols_one, 0, weight_one, bias_first))
        hid_halo("start", 0)

    mean_two, scale_two = scale_of(1, gain_second)
    hid_halo("recv", 1)
    spread_hidden(cols_two, 2, 1, mean_two, scale_two, shift_second)

    @pl.when(ta > 0)
    def _():
        hid_halo("recv", 0)
        spread_hidden(cols_two, 0, 0, mean_two, scale_two, shift_second)

    load_w2.wait()
    pair = conv_pair(cols_two, 0, weight_two, bias_second)
    for f, value in enumerate(pair):
        source = raw[2, f, 1 : rows + 1, PAD : PAD + cols, :].astype(jnp.float32)
        out[f] = (value.reshape(rows, cols, chans) + source).astype(out.dtype)

    for step in steps:

        @pl.when(ta + step < nta)
        def _():
            for copy in time_copies(step):
                copy.wait_send()

    raw_halo("send", 2)
    raw_halo("send", 1)

    @pl.when(ta > 0)
    def _():
        raw_halo("send", 0)

    hid_halo("send", 1)
    hid_halo("send", 0)
    for which in range(2):
        pltpu.make_async_copy(stat_in.at[which], stat_in.at[which], stat_send.at[which]).wait()


def on_device(
    sizes,
    frames,
    past_first,
    past_second,
    gain_first,
    shift_first,
    kernel_first,
    bias_first,
    gain_second,
    shift_second,
    kernel_second,
    bias_second,
):
    nframe, rows, cols, chans = frames.shape
    nha, nwa, nta = sizes
    peers = nha * nwa * nta
    line = lambda v: v.reshape(1, chans)
    stack = lambda k: k.reshape(3, 9 * chans, chans)
    bf16, f32 = jnp.bfloat16, jnp.float32
    anywhere = pl.BlockSpec(memory_space=pl.ANY)
    vmem = pl.BlockSpec(memory_space=pltpu.VMEM)
    dma = pltpu.SemaphoreType.DMA
    padded = (rows + 2, cols + 2 * PAD, chans)
    sides = len(DIRECTIONS)
    return pl.pallas_call(
        functools.partial(body, sizes),
        out_shape=jax.ShapeDtypeStruct(frames.shape, bf16),
        in_specs=[anywhere] * 3 + [vmem, vmem, anywhere, vmem] * 2,
        out_specs=vmem,
        scratch_shapes=[
            pltpu.VMEM((3, nframe) + padded, bf16),
            pltpu.VMEM((2, nframe) + padded, bf16),
            pltpu.VMEM((2, nframe, rows, cols, chans), f32),
            pltpu.VMEM((cols + 2 * PAD, chans), f32),
            pltpu.VMEM((3 * nframe, rows + 2, cols, 3 * chans), bf16),
            pltpu.VMEM((2 * nframe, rows + 2, cols, 3 * chans), bf16),
            pltpu.VMEM((3, 9 * chans, chans), bf16),
            pltpu.VMEM((3, 9 * chans, chans), bf16),
            pltpu.VMEM((2, 2, chans), f32),
            pltpu.VMEM((2, peers - 1, 2, chans), f32),
            dma((5,)),
            dma((3, sides)),
            dma((3, sides)),
            dma((2, sides)),
            dma((2, sides)),
            dma((2, 3)),
            dma((2, 3)),
            dma((2,)),
            dma((2,)),
        ],
        compiler_params=pltpu.CompilerParams(
            collective_id=0, has_side_effects=True, vmem_limit_bytes=48 * 1024 * 1024
        ),
        cost_estimate=pl.CostEstimate(
            flops=4 * 27 * nframe * rows * cols * chans * chans,
            bytes_accessed=4 * 1024 * 1024,
            transcendentals=4 * nframe * rows * cols * chans,
        ),
    )(
        frames,
        past_first,
        past_second,
        line(gain_first),
        line(shift_first),
        stack(kernel_first),
        line(bias_first),
        line(gain_second),
        line(shift_second),
        stack(kernel_second),
        line(bias_second),
    )


def solution(mesh):
    sizes = tuple(mesh.shape[name] for name in ("ha", "wa", "ta"))
    return jax.shard_map(
        functools.partial(on_device, sizes),
        mesh=mesh,
        in_specs=(
            P(("clips", "ta"), "ha", "wa", None),
            P("clips", "ha", "wa", None),
            P("clips", "ha", "wa", None),
        )
        + (P(),) * 8,
        out_specs=P(("clips", "ta"), "ha", "wa", None),
        check_vma=False,
    )
```

```python
import functools

import jax
import jax.numpy as jnp
from jax import lax
from jax.experimental import pallas as pl
from jax.experimental.pallas import tpu as pltpu
from jax.sharding import PartitionSpec as P

EPS = 1e-06
G = 32
PAD = 16
MESH = pl.DeviceIdType.MESH
DIRECTIONS = [(dh, dw) for dh in (-1, 0, 1) for dw in (-1, 0, 1) if (dh, dw) != (0, 0)]


def body(
    sizes,
    frames,
    past_first,
    past_second,
    gain_first_in,
    shift_first_in,
    kernel_first,
    bias_first_in,
    gain_second_in,
    shift_second_in,
    kernel_second,
    bias_second_in,
    out,
    vectors,
    total,
    raw,
    hid_edge,
    hid,
    line,
    cols_one,
    cols_two,
    weight_one,
    weight_two,
    stat_own,
    stat_in,
    local_sem,
    raw_send,
    raw_recv,
    hid_send,
    hid_recv,
    time_send,
    time_recv,
    stat_send,
    stat_recv,
):
    nha, nwa, nta = sizes
    peers = nha * nwa * nta
    _, nframe, rows2, width, chans = raw.shape
    rows, cols = rows2 - 2, width - 2 * PAD
    ha, wa, ta = lax.axis_index("ha"), lax.axis_index("wa"), lax.axis_index("ta")
    me = (ha * nwa + wa) * nta + ta
    count = float(nframe * rows * cols * (chans // G) * peers)

    def place(k):
        other = lax.rem(me + k, peers)
        return {
            "ha": other // (nwa * nta),
            "wa": lax.rem(other // nta, nwa),
            "ta": lax.rem(other, nta),
        }

    def inner(buf, slot):
        return buf.at[slot, :, pl.ds(1, rows), pl.ds(PAD, cols), :]

    load_frames = pltpu.make_async_copy(frames, inner(raw, 2), local_sem.at[0])
    load_past = pltpu.make_async_copy(past_first, inner(raw, jnp.maximum(1 - ta, 0)), local_sem.at[1])
    load_second = pltpu.make_async_copy(past_second, inner(hid_edge, 0), local_sem.at[2])
    vector_in = (
        gain_first_in,
        shift_first_in,
        bias_first_in,
        gain_second_in,
        shift_second_in,
        bias_second_in,
    )
    load_vectors = [
        pltpu.make_async_copy(ref, vectors.at[i], local_sem.at[5 + i])
        for i, ref in enumerate(vector_in)
    ]
    gain_first, shift_first, bias_first, gain_second, shift_second, bias_second = (
        vectors.at[i] for i in range(6)
    )
    load_w1 = pltpu.make_async_copy(kernel_first, weight_one, local_sem.at[3])
    load_w2 = pltpu.make_async_copy(kernel_second, weight_two, local_sem.at[4])

    def halo_copy(buf, slot, send, recv, d):
        dh, dw = DIRECTIONS[d]
        row_from, row_to, nrow = {-1: (1, rows + 1, 1), 0: (1, 1, rows), 1: (rows, 0, 1)}[dh]
        col_from, col_to, ncol = {
            -1: (PAD, PAD + cols, PAD),
            0: (PAD, PAD, cols),
            1: (cols, 0, PAD),
        }[dw]
        copy = pltpu.make_async_remote_copy(
            src_ref=buf.at[slot, :, pl.ds(row_from, nrow), pl.ds(col_from, ncol), :],
            dst_ref=buf.at[slot, :, pl.ds(row_to, nrow), pl.ds(col_to, ncol), :],
            send_sem=send.at[slot, d],
            recv_sem=recv.at[slot, d],
            device_id={"ha": ha + dh, "wa": wa + dw},
            device_id_type=MESH,
        )
        to_h, to_w = ha + dh, wa + dw
        from_h, from_w = ha - dh, wa - dw
        goes = (to_h >= 0) & (to_h < nha) & (to_w >= 0) & (to_w < nwa)
        comes = (from_h >= 0) & (from_h < nha) & (from_w >= 0) & (from_w < nwa)
        return copy, goes, comes

    def halo(action, buf, slot, send, recv, beside):
        for d in range(len(DIRECTIONS)):
            if (DIRECTIONS[d][0] == 0) not in beside:
                continue
            copy, goes, comes = halo_copy(buf, slot, send, recv, d)
            if action == "start":
                pl.when(goes)(copy.start)
            elif action == "recv":
                pl.when(comes)(copy.wait_recv)
            else:
                pl.when(goes)(copy.wait_send)

    def raw_halo(action, slot, beside=(False, True)):
        halo(action, raw, slot, raw_send, raw_recv, beside)

    def hid_halo(action, slot):
        halo(action, hid_edge, slot, hid_send, hid_recv, (False, True))

    def time_copies(step):
        slot = 2 - step
        parts = ((1, 1), (rows, 1), (2, rows - 2))
        return [
            pltpu.make_async_remote_copy(
                src_ref=raw.at[2, :, pl.ds(first, n), pl.ds(PAD, cols), :],
                dst_ref=raw.at[slot, :, pl.ds(first, n), pl.ds(PAD, cols), :],
                send_sem=time_send.at[step - 1, i],
                recv_sem=time_recv.at[step - 1, i],
                device_id={"ta": ta + step},
                device_id_type=MESH,
            )
            for i, (first, n) in enumerate(parts)
        ]

    steps = [step for step in (1, 2) if step < nta]

    def stat_copy(which, k):
        return pltpu.make_async_remote_copy(
            src_ref=stat_own.at[which],
            dst_ref=stat_in.at[which, k - 1],
            send_sem=stat_send.at[which],
            recv_sem=stat_recv.at[which],
            device_id=place(k),
            device_id_type=MESH,
        )

    def send_stats(which):
        @pl.loop(1, peers)
        def _(k):
            stat_copy(which, k).start()

    def group_total(which):
        pltpu.make_async_copy(stat_in.at[which], stat_in.at[which], stat_recv.at[which]).wait()
        sums = stat_own[which] + jnp.sum(stat_in[which], axis=0)
        lane = lax.broadcasted_iota(jnp.int32, sums.shape, 1)
        for shift in (1, 2):
            low = lax.rem(lane, 2 * shift) < shift
            sums = sums + jnp.where(
                low, pltpu.roll(sums, chans - shift, 1), pltpu.roll(sums, shift, 1)
            )
        return sums

    def scale_of(which, gain):
        sums = group_total(which)
        mean = sums[0:1] / count
        inverse = lax.rsqrt(sums[1:2] / count - mean * mean + EPS)
        return mean, inverse * gain[...]

    def put_stats(which, first, second):
        stat_own[which, 0:1, :] = jnp.sum(first, axis=0, keepdims=True)
        stat_own[which, 1:2, :] = jnp.sum(second, axis=0, keepdims=True)

    def act(value, mean, scale, shift):
        half = (value - mean) * (0.5 * scale) + 0.5 * shift[...]
        return half + half * jnp.tanh(half)

    half_pad = PAD // 2

    def spread(dst, frame, row, left, mid, right):
        left = jnp.where(wa > 0, left, 0.0)
        right = jnp.where(wa < nwa - 1, right, 0.0)
        if row in (0, rows + 1):
            live = (ha > 0) if row == 0 else (ha < nha - 1)
            left, mid, right = (jnp.where(live, value, 0.0) for value in (left, mid, right))
        line[row, 0:half_pad] = left
        line[row, half_pad : half_pad + cols] = mid
        line[row, half_pad + cols : PAD + cols] = right
        before = line[row, half_pad - 1 : half_pad - 1 + cols]
        after = line[row, half_pad + 1 : half_pad + 1 + cols]
        dst[frame, row, :, 0:chans] = before.astype(jnp.bfloat16)
        dst[frame, row, :, chans : 2 * chans] = mid.astype(jnp.bfloat16)
        dst[frame, row, :, 2 * chans :] = after.astype(jnp.bfloat16)

    def edges(buf, slot, f, r):
        left = buf[slot, f, r, 0:PAD].astype(jnp.float32)[half_pad:]
        right = buf[slot, f, r, PAD + cols :].astype(jnp.float32)[:half_pad]
        return left, right

    def middle(buf, slot, f, r):
        return buf[slot, f, r, PAD : PAD + cols].astype(jnp.float32)

    def spread_frames(dst, base, buf, slot, change, own=None):
        @pl.loop(0, nframe)
        def _(f):
            for r in range(rows2):
                left, right = edges(buf, slot, f, r)
                if own is not None and 0 < r < rows + 1:
                    mid = own[slot, f, r - 1]
                else:
                    mid = middle(buf, slot, f, r)
                spread(dst, base + f, r, change(left), change(mid), change(right))

    def spread_plain(dst, base, buf, slot):
        spread_frames(dst, base, buf, slot, lambda value: value)

    def spread_act(dst, base, slot, mean, scale, shift):
        spread_frames(dst, base, raw, slot, lambda value: act(value, mean, scale, shift))

    def spread_hidden(dst, base, slot, mean, scale, shift):
        spread_frames(
            dst, base, hid_edge, slot, lambda value: act(value, mean, scale, shift), hid
        )

    def slab(src, f):
        return jnp.concatenate(
            [src[f, b : b + rows].reshape(rows * cols, 3 * chans) for b in range(3)], axis=1
        )

    def dot(left, right):
        return jnp.dot(left, right, preferred_element_type=jnp.float32)

    def shaped(*pair):
        return [value.reshape(rows, cols, chans) for value in pair]

    def head(src, base, weight):
        both = dot(slab(src, base + 1), jnp.concatenate([weight[1], weight[0]], axis=1))
        one = both[:, :chans] + dot(slab(src, base), weight[0])
        return shaped(one, both[:, chans:])

    def tail(src, base, weight):
        both = dot(slab(src, base + 2), jnp.concatenate([weight[2], weight[1]], axis=1))
        two = both[:, chans:] + dot(slab(src, base + 3), weight[2])
        return shaped(both[:, :chans], two)

    def keep_edges(slot, pair):
        for f, value in enumerate(pair):
            hid_edge[slot, f, 1 : rows + 1, PAD : PAD + cols, :] = value.astype(jnp.bfloat16)

    load_frames.start()

    @pl.when(ta < 2)
    def _():
        load_past.start()

    @pl.when(ta == 0)
    def _():
        load_second.start()

    barrier = pltpu.get_barrier_semaphore()

    @pl.loop(1, peers)
    def _(k):
        pl.semaphore_signal(barrier, inc=1, device_id=place(k), device_id_type=MESH)

    for copy in load_vectors:
        copy.start()
    load_w1.start()
    load_w2.start()
    load_frames.wait()
    first = jnp.zeros((cols, chans), jnp.float32)
    second = jnp.zeros((cols, chans), jnp.float32)
    for f in range(nframe):
        for r in range(rows):
            value = raw[2, f, 1 + r, PAD : PAD + cols, :].astype(jnp.float32)
            first = first + value
            second = second + value * value
    put_stats(0, first, second)
    for copy in load_vectors:
        copy.wait()
    pl.semaphore_wait(barrier, peers - 1)

    for step in steps:

        @pl.when(ta + step < nta)
        def _():
            for copy in time_copies(step):
                copy.start()

    send_stats(0)
    raw_halo("start", 2)

    @pl.when(ta == 0)
    def _():
        load_past.wait()
        raw_halo("start", 1)
        load_second.wait()
        hid_halo("start", 0)

    @pl.when(ta == 1)
    def _():
        load_past.wait()
        raw_halo("start", 0)

    mean_one, scale_one = scale_of(0, gain_first)
    raw_halo("recv", 2)
    spread_act(cols_one, 4, 2, mean_one, scale_one, shift_first)
    load_w1.wait()
    for f, value in enumerate(tail(cols_one, 2, weight_one)):
        hid[1, f] = value + bias_first[...]

    @pl.when(ta == 0)
    def _():
        raw_halo("recv", 1)
        spread_plain(cols_one, 2, raw, 1)

    def past_part():
        for f, value in enumerate(head(cols_one, 0, weight_one)):
            hid[0, f] = value + bias_first[...]

    @pl.when(ta > 0)
    def _():
        def arrive(step):
            for copy in time_copies(step)[:2]:
                copy.wait_recv()
            raw_halo("start", 2 - step, (False,))

        def arrive_all(step):
            time_copies(step)[2].wait_recv()
            raw_halo("start", 2 - step, (True,))

        @pl.when(ta == 1)
        def _():
            raw_halo("recv", 0)
            spread_plain(cols_one, 0, raw, 0)

        arrive(1)

        @pl.when(ta == 1)
        def _():
            past_part()

        arrive_all(1)
        if nta > 2:

            @pl.when(ta > 1)
            def _():
                arrive(2)
                arrive_all(2)
                raw_halo("recv", 0)
                spread_act(cols_one, 0, 0, mean_one, scale_one, shift_first)
                past_part()

        raw_halo("recv", 1)
        spread_act(cols_one, 2, 1, mean_one, scale_one, shift_first)

    pair = head(cols_one, 2, weight_one)
    pair = [value + hid[1, f] for f, value in enumerate(pair)]
    flat = [value.reshape(rows * cols, chans) for value in pair]
    put_stats(1, flat[0] + flat[1], flat[0] * flat[0] + flat[1] * flat[1])
    send_stats(1)
    for f, value in enumerate(pair):
        hid[1, f] = value
    keep_edges(1, pair)
    hid_halo("start", 1)
    load_w2.wait()
    for f in range(nframe):
        total[f] = middle(raw, 2, f, slice(1, rows + 1)) + bias_second[...]

    def carried_part():
        for f, value in enumerate(head(cols_two, 0, weight_two)):
            total[f] += value

    @pl.when(ta > 0)
    def _():
        pair = tail(cols_one, 0, weight_one)
        pair = [value + hid[0, f] for f, value in enumerate(pair)]
        for f, value in enumerate(pair):
            hid[0, f] = value
        keep_edges(0, pair)
        hid_halo("start", 0)

    @pl.when(ta == 0)
    def _():
        hid_halo("recv", 0)
        spread_plain(cols_two, 0, hid_edge, 0)
        carried_part()

    mean_two, scale_two = scale_of(1, gain_second)
    hid_halo("recv", 1)
    spread_hidden(cols_two, 2, 1, mean_two, scale_two, shift_second)
    for f, value in enumerate(tail(cols_two, 0, weight_two)):
        total[f] += value

    @pl.when(ta > 0)
    def _():
        hid_halo("recv", 0)
        spread_hidden(cols_two, 0, 0, mean_two, scale_two, shift_second)
        carried_part()

    for f in range(nframe):
        out[f] = total[f].astype(out.dtype)

    for step in steps:

        @pl.when(ta + step < nta)
        def _():
            for copy in time_copies(step):
                copy.wait_send()

    raw_halo("send", 2)
    raw_halo("send", 1)

    @pl.when(ta > 0)
    def _():
        raw_halo("send", 0)

    hid_halo("send", 1)
    hid_halo("send", 0)
    for which in range(2):
        pltpu.make_async_copy(stat_in.at[which], stat_in.at[which], stat_send.at[which]).wait()


def on_device(
    sizes,
    frames,
    past_first,
    past_second,
    gain_first,
    shift_first,
    kernel_first,
    bias_first,
    gain_second,
    shift_second,
    kernel_second,
    bias_second,
):
    nframe, rows, cols, chans = frames.shape
    nha, nwa, nta = sizes
    peers = nha * nwa * nta
    line = lambda v: v.reshape(1, chans)
    stack = lambda k: k.reshape(3, 9 * chans, chans)
    bf16, f32 = jnp.bfloat16, jnp.float32
    hbm = pl.BlockSpec(memory_space=pltpu.HBM)
    vmem = pl.BlockSpec(memory_space=pltpu.VMEM)
    dma = pltpu.SemaphoreType.DMA
    padded = (rows + 2, cols + 2 * PAD, chans)
    sides = len(DIRECTIONS)
    return pl.pallas_call(
        functools.partial(body, sizes),
        out_shape=jax.ShapeDtypeStruct(frames.shape, bf16),
        in_specs=[hbm] * 11,
        out_specs=vmem,
        scratch_shapes=[
            pltpu.VMEM((6, 1, chans), f32),
            pltpu.VMEM((nframe, rows, cols, chans), f32),
            pltpu.VMEM((3, nframe) + padded, bf16),
            pltpu.VMEM((2, nframe) + padded, bf16),
            pltpu.VMEM((2, nframe, rows, cols, chans), f32),
            pltpu.VMEM((rows + 2, cols + PAD, chans), f32),
            pltpu.VMEM((3 * nframe, rows + 2, cols, 3 * chans), bf16),
            pltpu.VMEM((2 * nframe, rows + 2, cols, 3 * chans), bf16),
            pltpu.VMEM((3, 9 * chans, chans), bf16),
            pltpu.VMEM((3, 9 * chans, chans), bf16),
            pltpu.VMEM((2, 2, chans), f32),
            pltpu.VMEM((2, peers - 1, 2, chans), f32),
            dma((11,)),
            dma((3, sides)),
            dma((3, sides)),
            dma((2, sides)),
            dma((2, sides)),
            dma((2, 3)),
            dma((2, 3)),
            dma((2,)),
            dma((2,)),
        ],
        compiler_params=pltpu.CompilerParams(
            collective_id=0, has_side_effects=True, vmem_limit_bytes=62 * 1024 * 1024
        ),
        cost_estimate=pl.CostEstimate(
            flops=4 * 27 * nframe * rows * cols * chans * chans,
            bytes_accessed=4 * 1024 * 1024,
            transcendentals=4 * nframe * rows * cols * chans,
        ),
    )(
        frames,
        past_first,
        past_second,
        line(gain_first),
        line(shift_first),
        stack(kernel_first),
        line(bias_first),
        line(gain_second),
        line(shift_second),
        stack(kernel_second),
        line(bias_second),
    )


def solution(mesh):
    sizes = tuple(mesh.shape[name] for name in ("ha", "wa", "ta"))
    return jax.shard_map(
        functools.partial(on_device, sizes),
        mesh=mesh,
        in_specs=(
            P(("clips", "ta"), "ha", "wa", None),
            P("clips", "ha", "wa", None),
            P("clips", "ha", "wa", None),
        )
        + (P(),) * 8,
        out_specs=P(("clips", "ta"), "ha", "wa", None),
        check_vma=False,
    )
```

```python
import functools

import jax
import jax.numpy as jnp
from jax import lax
from jax.experimental import pallas as pl
from jax.experimental.pallas import tpu as pltpu
from jax.sharding import PartitionSpec as P

EPS = 1e-06
G = 32
PAD = 16
MESH = pl.DeviceIdType.MESH
DIRECTIONS = [(dh, dw) for dh in (-1, 0, 1) for dw in (-1, 0, 1) if (dh, dw) != (0, 0)]


def body(
    sizes,
    frames,
    past_first,
    past_second,
    gain_first_in,
    shift_first_in,
    kernel_first,
    bias_first_in,
    gain_second_in,
    shift_second_in,
    kernel_second,
    bias_second_in,
    out,
    vectors,
    total,
    raw,
    hid_edge,
    hid,
    line,
    cols_one,
    cols_two,
    weight_one,
    weight_two,
    stat_own,
    stat_in,
    local_sem,
    raw_send,
    raw_recv,
    hid_send,
    hid_recv,
    time_send,
    time_recv,
    col_send,
    col_recv,
    stat_send,
    stat_recv,
):
    nha, nwa, nta = sizes
    peers = nha * nwa * nta
    _, nframe, rows2, width, chans = raw.shape
    rows, cols = rows2 - 2, width - 2 * PAD
    ha, wa, ta = lax.axis_index("ha"), lax.axis_index("wa"), lax.axis_index("ta")
    count = float(nframe * rows * cols * (chans // G) * peers)

    def ring(at, step, size):
        return jnp.where(at + step >= size, at + step - size, at + step)

    def place(k):
        dh, dw, dt = k // (nwa * nta), k // nta % nwa, k % nta
        return {"ha": ring(ha, dh, nha), "wa": ring(wa, dw, nwa), "ta": ring(ta, dt, nta)}

    def each_peer(work):
        if peers <= 32:
            for k in range(1, peers):
                work(k)
        else:
            pl.loop(1, peers)(work)

    def inner(buf, slot):
        return buf.at[slot, :, pl.ds(1, rows), pl.ds(PAD, cols), :]

    load_frames = pltpu.make_async_copy(frames, inner(raw, 2), local_sem.at[0])
    load_past = pltpu.make_async_copy(past_first, inner(raw, jnp.maximum(1 - ta, 0)), local_sem.at[1])
    load_second = pltpu.make_async_copy(past_second, inner(hid_edge, 0), local_sem.at[2])
    vector_in = (
        gain_first_in,
        shift_first_in,
        bias_first_in,
        gain_second_in,
        shift_second_in,
        bias_second_in,
    )
    load_vectors = [
        pltpu.make_async_copy(ref, vectors.at[i, 0], local_sem.at[5 + i])
        for i, ref in enumerate(vector_in)
    ]
    gain_first, shift_first, bias_first, gain_second, shift_second, bias_second = (
        vectors.at[i] for i in range(6)
    )
    load_w1 = pltpu.make_async_copy(kernel_first, weight_one, local_sem.at[3])
    load_w2 = pltpu.make_async_copy(kernel_second, weight_two, local_sem.at[4])

    def halo_copy(buf, slot, send, recv, d):
        dh, dw = DIRECTIONS[d]
        row_from, row_to, nrow = {-1: (1, rows + 1, 1), 0: (1, 1, rows), 1: (rows, 0, 1)}[dh]
        col_from, col_to, ncol = {
            -1: (PAD, PAD + cols, PAD),
            0: (PAD, PAD, cols),
            1: (cols, 0, PAD),
        }[dw]
        copy = pltpu.make_async_remote_copy(
            src_ref=buf.at[slot, :, pl.ds(row_from, nrow), pl.ds(col_from, ncol), :],
            dst_ref=buf.at[slot, :, pl.ds(row_to, nrow), pl.ds(col_to, ncol), :],
            send_sem=send.at[slot, d],
            recv_sem=recv.at[slot, d],
            device_id={"ha": ha + dh, "wa": wa + dw},
            device_id_type=MESH,
        )
        to_h, to_w = ha + dh, wa + dw
        from_h, from_w = ha - dh, wa - dw
        goes = (to_h >= 0) & (to_h < nha) & (to_w >= 0) & (to_w < nwa)
        comes = (from_h >= 0) & (from_h < nha) & (from_w >= 0) & (from_w < nwa)
        return copy, goes, comes

    def halo(action, buf, slot, send, recv, beside):
        for d in range(len(DIRECTIONS)):
            if (DIRECTIONS[d][0] == 0) not in beside:
                continue
            copy, goes, comes = halo_copy(buf, slot, send, recv, d)
            if action == "start":
                pl.when(goes)(copy.start)
            elif action == "recv":
                pl.when(comes)(copy.wait_recv)
            else:
                pl.when(goes)(copy.wait_send)

    def raw_halo(action, slot, beside=(False, True)):
        halo(action, raw, slot, raw_send, raw_recv, beside)

    def hid_halo(action, slot):
        halo(action, hid_edge, slot, hid_send, hid_recv, (False, True))

    row_parts = ((1, 1), (rows, 1), (2, rows - 2))

    def time_copies(step):
        slot = 2 - step
        return [
            pltpu.make_async_remote_copy(
                src_ref=raw.at[2, :, pl.ds(first, n), pl.ds(PAD, cols), :],
                dst_ref=raw.at[slot, :, pl.ds(first, n), pl.ds(PAD, cols), :],
                send_sem=time_send.at[step - 1, i],
                recv_sem=time_recv.at[step - 1, i],
                device_id={"ta": ta + step},
                device_id_type=MESH,
            )
            for i, (first, n) in enumerate(row_parts)
        ]

    def column_relays(action, part):
        first, n = row_parts[part]
        for side, dw in enumerate((-1, 1)):
            col_from, col_to = (PAD, PAD + cols) if dw < 0 else (cols, 0)
            copy = pltpu.make_async_remote_copy(
                src_ref=raw.at[1, :, pl.ds(first, n), pl.ds(col_from, PAD), :],
                dst_ref=raw.at[1, :, pl.ds(first, n), pl.ds(col_to, PAD), :],
                send_sem=col_send.at[part, side],
                recv_sem=col_recv.at[part, side],
                device_id={"wa": wa + dw},
                device_id_type=MESH,
            )
            goes = (wa + dw >= 0) & (wa + dw < nwa)
            comes = (wa - dw >= 0) & (wa - dw < nwa)
            if action == "start":
                pl.when(goes)(copy.start)
            elif action == "recv":
                pl.when(comes)(copy.wait_recv)
            else:
                pl.when(goes)(copy.wait_send)

    steps = [step for step in (1, 2) if step < nta]

    def stat_copy(which, k):
        return pltpu.make_async_remote_copy(
            src_ref=stat_own.at[which],
            dst_ref=stat_in.at[which, k - 1],
            send_sem=stat_send.at[which],
            recv_sem=stat_recv.at[which],
            device_id=place(k),
            device_id_type=MESH,
        )

    def send_stats(which):
        each_peer(lambda k: stat_copy(which, k).start())

    def group_total(which):
        pltpu.make_async_copy(stat_in.at[which], stat_in.at[which], stat_recv.at[which]).wait()
        sums = stat_own[which] + jnp.sum(stat_in[which], axis=0)
        lane = lax.broadcasted_iota(jnp.int32, sums.shape, 1)
        for shift in (1, 2):
            low = lax.rem(lane, 2 * shift) < shift
            sums = sums + jnp.where(
                low, pltpu.roll(sums, chans - shift, 1), pltpu.roll(sums, shift, 1)
            )
        return sums

    def scale_of(which, gain):
        sums = group_total(which)
        mean = sums[0:1] / count
        inverse = lax.rsqrt(sums[1:2] / count - mean * mean + EPS)
        return mean, inverse * gain[...]

    def put_stats(which, first, second):
        stat_own[which, 0:1, :] = jnp.sum(first, axis=0, keepdims=True)
        stat_own[which, 1:2, :] = jnp.sum(second, axis=0, keepdims=True)

    def act(value, mean, scale, shift):
        half = (value - mean) * (0.5 * scale) + 0.5 * shift[...]
        return half + half * jnp.tanh(half)

    half_pad = PAD // 2

    def spread(dst, frame, row, left, mid, right):
        left = jnp.where(wa > 0, left, 0.0)
        right = jnp.where(wa < nwa - 1, right, 0.0)
        if row in (0, rows + 1):
            live = (ha > 0) if row == 0 else (ha < nha - 1)
            left, mid, right = (jnp.where(live, value, 0.0) for value in (left, mid, right))
        line[row, 0:half_pad] = left
        line[row, half_pad : half_pad + cols] = mid
        line[row, half_pad + cols : PAD + cols] = right
        before = line[row, half_pad - 1 : half_pad - 1 + cols]
        after = line[row, half_pad + 1 : half_pad + 1 + cols]
        dst[frame, row, :, 0:chans] = before.astype(jnp.bfloat16)
        dst[frame, row, :, chans : 2 * chans] = mid.astype(jnp.bfloat16)
        dst[frame, row, :, 2 * chans :] = after.astype(jnp.bfloat16)

    def edges(buf, slot, f, r):
        left = buf[slot, f, r, 0:PAD].astype(jnp.float32)[half_pad:]
        right = buf[slot, f, r, PAD + cols :].astype(jnp.float32)[:half_pad]
        return left, right

    def middle(buf, slot, f, r):
        return buf[slot, f, r, PAD : PAD + cols].astype(jnp.float32)

    def spread_frames(dst, base, buf, slot, change, own=None, which=None):
        @pl.loop(0, nframe)
        def _(f):
            for r in which or range(rows2):
                left, right = edges(buf, slot, f, r)
                if own is not None and 0 < r < rows + 1:
                    mid = own[slot, f, r - 1]
                else:
                    mid = middle(buf, slot, f, r)
                spread(dst, base + f, r, change(left), change(mid), change(right))

    def spread_plain(dst, base, buf, slot):
        spread_frames(dst, base, buf, slot, lambda value: value)

    def spread_act(dst, base, slot, mean, scale, shift, which=None):
        spread_frames(
            dst, base, raw, slot, lambda value: act(value, mean, scale, shift), None, which
        )

    def spread_hidden(dst, base, slot, mean, scale, shift):
        spread_frames(
            dst, base, hid_edge, slot, lambda value: act(value, mean, scale, shift), hid
        )

    def slab(src, f):
        return jnp.concatenate(
            [src[f, b : b + rows].reshape(rows * cols, 3 * chans) for b in range(3)], axis=1
        )

    def dot(left, right):
        return jnp.dot(left, right, preferred_element_type=jnp.float32)

    def shaped(*pair):
        return [value.reshape(rows, cols, chans) for value in pair]

    def head(src, base, weight):
        both = dot(slab(src, base + 1), jnp.concatenate([weight[1], weight[0]], axis=1))
        one = both[:, :chans] + dot(slab(src, base), weight[0])
        return shaped(one, both[:, chans:])

    def tail(src, base, weight):
        both = dot(slab(src, base + 2), jnp.concatenate([weight[2], weight[1]], axis=1))
        two = both[:, chans:] + dot(slab(src, base + 3), weight[2])
        return shaped(both[:, :chans], two)

    def keep_edges(slot, pair):
        for f, value in enumerate(pair):
            hid_edge[slot, f, 1 : rows + 1, PAD : PAD + cols, :] = value.astype(jnp.bfloat16)

    load_frames.start()

    @pl.when(ta < 2)
    def _():
        load_past.start()

    @pl.when(ta == 0)
    def _():
        load_second.start()

    barrier = pltpu.get_barrier_semaphore()

    each_peer(
        lambda k: pl.semaphore_signal(barrier, inc=1, device_id=place(k), device_id_type=MESH)
    )

    for copy in load_vectors:
        copy.start()
    load_w1.start()
    load_w2.start()
    load_frames.wait()
    first = jnp.zeros((cols, chans), jnp.float32)
    second = jnp.zeros((cols, chans), jnp.float32)
    for f in range(nframe):
        for r in range(rows):
            value = raw[2, f, 1 + r, PAD : PAD + cols, :].astype(jnp.float32)
            first = first + value
            second = second + value * value
    put_stats(0, first, second)
    for copy in load_vectors:
        copy.wait()
    pl.semaphore_wait(barrier, peers - 1)

    for step in steps:

        @pl.when(ta + step < nta)
        def _():
            for copy in time_copies(step):
                copy.start()

    send_stats(0)
    raw_halo("start", 2)

    @pl.when(ta == 0)
    def _():
        load_past.wait()
        raw_halo("start", 1)

    @pl.when(ta == 1)
    def _():
        load_past.wait()
        raw_halo("start", 0)

    mean_one, scale_one = scale_of(0, gain_first)
    raw_halo("recv", 2)
    spread_act(cols_one, 4, 2, mean_one, scale_one, shift_first)
    load_w1.wait()
    for f, value in enumerate(tail(cols_one, 2, weight_one)):
        hid[1, f] = value + bias_first[...]

    @pl.when(ta == 0)
    def _():
        load_second.wait()
        hid_halo("start", 0)
        raw_halo("recv", 1)
        spread_plain(cols_one, 2, raw, 1)

    def past_part():
        for f, value in enumerate(head(cols_one, 0, weight_one)):
            hid[0, f] = value + bias_first[...]

    @pl.when(ta > 0)
    def _():
        @pl.when(ta == 1)
        def _():
            raw_halo("recv", 0)
            spread_plain(cols_one, 0, raw, 0)

        near = time_copies(1)
        for part in (0, 1):
            near[part].wait_recv()
            column_relays("start", part)
        raw_halo("start", 1, (False,))

        @pl.when(ta == 1)
        def _():
            past_part()

        def carried(which):
            spread_act(cols_one, 2, 1, mean_one, scale_one, shift_first, which)

        column_relays("recv", 0)
        column_relays("recv", 1)
        carried((1, rows))
        near[2].wait_recv()
        column_relays("start", 2)
        raw_halo("recv", 1, (False,))
        carried((0, rows + 1))
        column_relays("recv", 2)
        carried(tuple(range(2, rows)))
        if nta > 2:

            @pl.when(ta > 1)
            def _():
                for copy in time_copies(2):
                    copy.wait_recv()
                raw_halo("start", 0)
                raw_halo("recv", 0)
                spread_act(cols_one, 0, 0, mean_one, scale_one, shift_first)
                past_part()

    pair = head(cols_one, 2, weight_one)
    pair = [value + hid[1, f] for f, value in enumerate(pair)]
    flat = [value.reshape(rows * cols, chans) for value in pair]
    put_stats(1, flat[0] + flat[1], flat[0] * flat[0] + flat[1] * flat[1])
    send_stats(1)
    for f, value in enumerate(pair):
        hid[1, f] = value
    keep_edges(1, pair)
    hid_halo("start", 1)
    load_w2.wait()
    for f in range(nframe):
        total[f] = middle(raw, 2, f, slice(1, rows + 1)) + bias_second[...]

    def carried_part():
        for f, value in enumerate(head(cols_two, 0, weight_two)):
            total[f] += value

    @pl.when(ta > 0)
    def _():
        pair = tail(cols_one, 0, weight_one)
        pair = [value + hid[0, f] for f, value in enumerate(pair)]
        for f, value in enumerate(pair):
            hid[0, f] = value
        keep_edges(0, pair)
        hid_halo("start", 0)

    @pl.when(ta == 0)
    def _():
        hid_halo("recv", 0)
        spread_plain(cols_two, 0, hid_edge, 0)
        carried_part()

    mean_two, scale_two = scale_of(1, gain_second)
    hid_halo("recv", 1)
    spread_hidden(cols_two, 2, 1, mean_two, scale_two, shift_second)
    for f, value in enumerate(tail(cols_two, 0, weight_two)):
        total[f] += value

    @pl.when(ta > 0)
    def _():
        hid_halo("recv", 0)
        spread_hidden(cols_two, 0, 0, mean_two, scale_two, shift_second)
        carried_part()

    for f in range(nframe):
        out[f] = total[f].astype(out.dtype)

    for step in steps:

        @pl.when(ta + step < nta)
        def _():
            for copy in time_copies(step):
                copy.wait_send()

    raw_halo("send", 2)
    raw_halo("send", 1, (False,))

    @pl.when(ta == 0)
    def _():
        raw_halo("send", 1, (True,))

    @pl.when(ta > 0)
    def _():
        for part in range(3):
            column_relays("send", part)
        raw_halo("send", 0)

    hid_halo("send", 1)
    hid_halo("send", 0)
    for which in range(2):
        pltpu.make_async_copy(stat_in.at[which], stat_in.at[which], stat_send.at[which]).wait()


def on_device(
    sizes,
    frames,
    past_first,
    past_second,
    gain_first,
    shift_first,
    kernel_first,
    bias_first,
    gain_second,
    shift_second,
    kernel_second,
    bias_second,
):
    nframe, rows, cols, chans = frames.shape
    nha, nwa, nta = sizes
    peers = nha * nwa * nta
    line = lambda v: v
    stack = lambda k: k.reshape(3, 9 * chans, chans)
    bf16, f32 = jnp.bfloat16, jnp.float32
    hbm = pl.BlockSpec(memory_space=pltpu.HBM)
    vmem = pl.BlockSpec(memory_space=pltpu.VMEM)
    dma = pltpu.SemaphoreType.DMA
    padded = (rows + 2, cols + 2 * PAD, chans)
    sides = len(DIRECTIONS)
    return pl.pallas_call(
        functools.partial(body, sizes),
        out_shape=jax.ShapeDtypeStruct(frames.shape, bf16),
        in_specs=[hbm] * 11,
        out_specs=vmem,
        scratch_shapes=[
            pltpu.VMEM((6, 1, chans), f32),
            pltpu.VMEM((nframe, rows, cols, chans), f32),
            pltpu.VMEM((3, nframe) + padded, bf16),
            pltpu.VMEM((2, nframe) + padded, bf16),
            pltpu.VMEM((2, nframe, rows, cols, chans), f32),
            pltpu.VMEM((rows + 2, cols + PAD, chans), f32),
            pltpu.VMEM((3 * nframe, rows + 2, cols, 3 * chans), bf16),
            pltpu.VMEM((2 * nframe, rows + 2, cols, 3 * chans), bf16),
            pltpu.VMEM((3, 9 * chans, chans), bf16),
            pltpu.VMEM((3, 9 * chans, chans), bf16),
            pltpu.VMEM((2, 2, chans), f32),
            pltpu.VMEM((2, peers - 1, 2, chans), f32),
            dma((11,)),
            dma((3, sides)),
            dma((3, sides)),
            dma((2, sides)),
            dma((2, sides)),
            dma((2, 3)),
            dma((2, 3)),
            dma((3, 2)),
            dma((3, 2)),
            dma((2,)),
            dma((2,)),
        ],
        compiler_params=pltpu.CompilerParams(
            collective_id=0, has_side_effects=True, vmem_limit_bytes=62 * 1024 * 1024
        ),
        cost_estimate=pl.CostEstimate(
            flops=4 * 27 * nframe * rows * cols * chans * chans,
            bytes_accessed=4 * 1024 * 1024,
            transcendentals=4 * nframe * rows * cols * chans,
        ),
    )(
        frames,
        past_first,
        past_second,
        line(gain_first),
        line(shift_first),
        stack(kernel_first),
        line(bias_first),
        line(gain_second),
        line(shift_second),
        stack(kernel_second),
        line(bias_second),
    )


def solution(mesh):
    sizes = tuple(mesh.shape[name] for name in ("ha", "wa", "ta"))
    return jax.shard_map(
        functools.partial(on_device, sizes),
        mesh=mesh,
        in_specs=(
            P(("clips", "ta"), "ha", "wa", None),
            P("clips", "ha", "wa", None),
            P("clips", "ha", "wa", None),
        )
        + (P(),) * 8,
        out_specs=P(("clips", "ta"), "ha", "wa", None),
        check_vma=False,
    )
```

```python
import functools

import jax
import jax.numpy as jnp
from jax import lax
from jax.experimental import pallas as pl
from jax.experimental.pallas import tpu as pltpu
from jax.sharding import PartitionSpec as P

EPS = 1e-06
G = 32
PAD = 16
MESH = pl.DeviceIdType.MESH
DIRECTIONS = [(dh, dw) for dh in (-1, 0, 1) for dw in (-1, 0, 1) if (dh, dw) != (0, 0)]


def body(
    sizes,
    frames,
    past_first,
    past_second,
    gain_first_in,
    shift_first_in,
    kernel_first,
    bias_first_in,
    gain_second_in,
    shift_second_in,
    kernel_second,
    bias_second_in,
    out,
    vectors,
    total,
    raw,
    hid_edge,
    hid,
    line,
    cols_one,
    cols_two,
    weight_one,
    weight_two,
    stat_own,
    stat_in,
    local_sem,
    raw_send,
    raw_recv,
    hid_send,
    hid_recv,
    time_send,
    time_recv,
    col_send,
    col_recv,
    stat_send,
    stat_recv,
):
    nha, nwa, nta = sizes
    peers = nha * nwa * nta
    _, nframe, rows2, width, chans = raw.shape
    rows, cols = rows2 - 2, width - 2 * PAD
    ha, wa, ta = lax.axis_index("ha"), lax.axis_index("wa"), lax.axis_index("ta")
    count = float(nframe * rows * cols * (chans // G) * peers)

    def ring(at, step, size):
        return jnp.where(at + step >= size, at + step - size, at + step)

    def place(k):
        dh, dw, dt = k // (nwa * nta), k // nta % nwa, k % nta
        return {"ha": ring(ha, dh, nha), "wa": ring(wa, dw, nwa), "ta": ring(ta, dt, nta)}

    def each_peer(work):
        if peers <= 32:
            for k in range(1, peers):
                work(k)
        else:
            pl.loop(1, peers)(work)

    def inner(buf, slot):
        return buf.at[slot, :, pl.ds(1, rows), pl.ds(PAD, cols), :]

    load_frames = pltpu.make_async_copy(frames, inner(raw, 2), local_sem.at[0])
    load_past = pltpu.make_async_copy(past_first, inner(raw, jnp.maximum(1 - ta, 0)), local_sem.at[1])
    load_second = pltpu.make_async_copy(past_second, inner(hid_edge, 0), local_sem.at[2])
    vector_in = (
        gain_first_in,
        shift_first_in,
        bias_first_in,
        gain_second_in,
        shift_second_in,
        bias_second_in,
    )
    load_vectors = [
        pltpu.make_async_copy(ref, vectors.at[i, 0], local_sem.at[5 + i])
        for i, ref in enumerate(vector_in)
    ]
    gain_first, shift_first, bias_first, gain_second, shift_second, bias_second = (
        vectors.at[i] for i in range(6)
    )
    load_w1 = pltpu.make_async_copy(kernel_first, weight_one, local_sem.at[3])
    load_w2 = pltpu.make_async_copy(kernel_second, weight_two, local_sem.at[4])

    def halo_copy(buf, slot, send, recv, d):
        dh, dw = DIRECTIONS[d]
        row_from, row_to, nrow = {-1: (1, rows + 1, 1), 0: (1, 1, rows), 1: (rows, 0, 1)}[dh]
        col_from, col_to, ncol = {
            -1: (PAD, PAD + cols, PAD),
            0: (PAD, PAD, cols),
            1: (cols, 0, PAD),
        }[dw]
        copy = pltpu.make_async_remote_copy(
            src_ref=buf.at[slot, :, pl.ds(row_from, nrow), pl.ds(col_from, ncol), :],
            dst_ref=buf.at[slot, :, pl.ds(row_to, nrow), pl.ds(col_to, ncol), :],
            send_sem=send.at[slot, d],
            recv_sem=recv.at[slot, d],
            device_id={"ha": ha + dh, "wa": wa + dw},
            device_id_type=MESH,
        )
        to_h, to_w = ha + dh, wa + dw
        from_h, from_w = ha - dh, wa - dw
        goes = (to_h >= 0) & (to_h < nha) & (to_w >= 0) & (to_w < nwa)
        comes = (from_h >= 0) & (from_h < nha) & (from_w >= 0) & (from_w < nwa)
        return copy, goes, comes

    def halo(action, buf, slot, send, recv, beside):
        for d in range(len(DIRECTIONS)):
            if (DIRECTIONS[d][0] == 0) not in beside:
                continue
            copy, goes, comes = halo_copy(buf, slot, send, recv, d)
            if action == "start":
                pl.when(goes)(copy.start)
            elif action == "recv":
                pl.when(comes)(copy.wait_recv)
            else:
                pl.when(goes)(copy.wait_send)

    def raw_halo(action, slot, beside=(False, True)):
        halo(action, raw, slot, raw_send, raw_recv, beside)

    def hid_halo(action, slot):
        halo(action, hid_edge, slot, hid_send, hid_recv, (False, True))

    row_parts = ((1, 1), (rows, 1), (2, rows - 2))

    def time_copies(step):
        slot = 2 - step
        return [
            pltpu.make_async_remote_copy(
                src_ref=raw.at[2, :, pl.ds(first, n), pl.ds(PAD, cols), :],
                dst_ref=raw.at[slot, :, pl.ds(first, n), pl.ds(PAD, cols), :],
                send_sem=time_send.at[step - 1, i],
                recv_sem=time_recv.at[step - 1, i],
                device_id={"ta": ta + step},
                device_id_type=MESH,
            )
            for i, (first, n) in enumerate(row_parts)
        ]

    def column_relays(action, part):
        first, n = row_parts[part]
        for side, dw in enumerate((-1, 1)):
            col_from, col_to = (PAD, PAD + cols) if dw < 0 else (cols, 0)
            copy = pltpu.make_async_remote_copy(
                src_ref=raw.at[1, :, pl.ds(first, n), pl.ds(col_from, PAD), :],
                dst_ref=raw.at[1, :, pl.ds(first, n), pl.ds(col_to, PAD), :],
                send_sem=col_send.at[part, side],
                recv_sem=col_recv.at[part, side],
                device_id={"wa": wa + dw},
                device_id_type=MESH,
            )
            goes = (wa + dw >= 0) & (wa + dw < nwa)
            comes = (wa - dw >= 0) & (wa - dw < nwa)
            if action == "start":
                pl.when(goes)(copy.start)
            elif action == "recv":
                pl.when(comes)(copy.wait_recv)
            else:
                pl.when(goes)(copy.wait_send)

    steps = [step for step in (1, 2) if step < nta]

    def stat_copy(which, k):
        return pltpu.make_async_remote_copy(
            src_ref=stat_own.at[which],
            dst_ref=stat_in.at[which, k - 1],
            send_sem=stat_send.at[which],
            recv_sem=stat_recv.at[which],
            device_id=place(k),
            device_id_type=MESH,
        )

    def send_stats(which):
        each_peer(lambda k: stat_copy(which, k).start())

    def group_total(which):
        pltpu.make_async_copy(stat_in.at[which], stat_in.at[which], stat_recv.at[which]).wait()
        sums = stat_own[which] + jnp.sum(stat_in[which], axis=0)
        lane = lax.broadcasted_iota(jnp.int32, sums.shape, 1)
        for shift in (1, 2):
            low = lax.rem(lane, 2 * shift) < shift
            sums = sums + jnp.where(
                low, pltpu.roll(sums, chans - shift, 1), pltpu.roll(sums, shift, 1)
            )
        return sums

    def scale_of(which, gain):
        sums = group_total(which)
        mean = sums[0:1] / count
        inverse = lax.rsqrt(sums[1:2] / count - mean * mean + EPS)
        return mean, inverse * gain[...]

    def put_stats(which, first, second):
        stat_own[which, 0:1, :] = jnp.sum(first, axis=0, keepdims=True)
        stat_own[which, 1:2, :] = jnp.sum(second, axis=0, keepdims=True)

    def act(value, mean, scale, shift):
        half = (value - mean) * (0.5 * scale) + 0.5 * shift[...]
        return half + half * jnp.tanh(half)

    half_pad = PAD // 2
    origin = jnp.minimum(ta, 0)

    def spread(dst, frame, row, left, mid, right):
        left = jnp.where(wa > 0, left, 0.0)
        right = jnp.where(wa < nwa - 1, right, 0.0)
        if row in (0, rows + 1):
            live = (ha > 0) if row == 0 else (ha < nha - 1)
            left, mid, right = (jnp.where(live, value, 0.0) for value in (left, mid, right))
        line[row, 0:half_pad] = left
        line[row, half_pad : half_pad + cols] = mid
        line[row, half_pad + cols : PAD + cols] = right
        before = line[row, pl.ds(half_pad - 1 + origin, cols)]
        after = line[row, pl.ds(half_pad + 1 + origin, cols)]
        dst[frame, row, :, 0:chans] = before.astype(jnp.bfloat16)
        dst[frame, row, :, chans : 2 * chans] = mid.astype(jnp.bfloat16)
        dst[frame, row, :, 2 * chans :] = after.astype(jnp.bfloat16)

    def edges(buf, slot, f, r):
        left = buf[slot, f, r, 0:PAD].astype(jnp.float32)[half_pad:]
        right = buf[slot, f, r, PAD + cols :].astype(jnp.float32)[:half_pad]
        return left, right

    def middle(buf, slot, f, r):
        return buf[slot, f, r, PAD : PAD + cols].astype(jnp.float32)

    def spread_frames(dst, base, buf, slot, change, own=None, which=None):
        @pl.loop(0, nframe)
        def _(f):
            for r in which or range(rows2):
                left, right = edges(buf, slot, f, r)
                if own is not None and 0 < r < rows + 1:
                    mid = own[slot, f, r - 1]
                else:
                    mid = middle(buf, slot, f, r)
                spread(dst, base + f, r, change(left), change(mid), change(right))

    def spread_plain(dst, base, buf, slot):
        spread_frames(dst, base, buf, slot, lambda value: value)

    def spread_act(dst, base, slot, mean, scale, shift, which=None):
        spread_frames(
            dst, base, raw, slot, lambda value: act(value, mean, scale, shift), None, which
        )

    def spread_hidden(dst, base, slot, mean, scale, shift):
        spread_frames(
            dst, base, hid_edge, slot, lambda value: act(value, mean, scale, shift), hid
        )

    def slab(src, f):
        return jnp.concatenate(
            [src[f, b : b + rows].reshape(rows * cols, 3 * chans) for b in range(3)], axis=1
        )

    def dot(left, right):
        return jnp.dot(left, right, preferred_element_type=jnp.float32)

    def shaped(*pair):
        return [value.reshape(rows, cols, chans) for value in pair]

    def head(src, base, weight):
        both = dot(slab(src, base + 1), jnp.concatenate([weight[1], weight[0]], axis=1))
        one = both[:, :chans] + dot(slab(src, base), weight[0])
        return shaped(one, both[:, chans:])

    def tail(src, base, weight):
        both = dot(slab(src, base + 2), jnp.concatenate([weight[2], weight[1]], axis=1))
        two = both[:, chans:] + dot(slab(src, base + 3), weight[2])
        return shaped(both[:, :chans], two)

    def keep_edges(slot, pair):
        for f, value in enumerate(pair):
            hid_edge[slot, f, 1 : rows + 1, PAD : PAD + cols, :] = value.astype(jnp.bfloat16)

    load_frames.start()

    @pl.when(ta < 2)
    def _():
        load_past.start()

    @pl.when(ta == 0)
    def _():
        load_second.start()

    barrier = pltpu.get_barrier_semaphore()

    each_peer(
        lambda k: pl.semaphore_signal(barrier, inc=1, device_id=place(k), device_id_type=MESH)
    )

    for copy in load_vectors:
        copy.start()
    load_w1.start()
    load_w2.start()
    load_frames.wait()
    first = jnp.zeros((cols, chans), jnp.float32)
    second = jnp.zeros((cols, chans), jnp.float32)
    for f in range(nframe):
        for r in range(rows):
            value = raw[2, f, 1 + r, PAD : PAD + cols, :].astype(jnp.float32)
            first = first + value
            second = second + value * value
    put_stats(0, first, second)
    for copy in load_vectors:
        copy.wait()
    pl.semaphore_wait(barrier, peers - 1)

    for step in steps:

        @pl.when(ta + step < nta)
        def _():
            for copy in time_copies(step):
                copy.start()

    send_stats(0)
    raw_halo("start", 2)

    @pl.when(ta == 0)
    def _():
        load_past.wait()
        raw_halo("start", 1)

    @pl.when(ta == 1)
    def _():
        load_past.wait()
        raw_halo("start", 0)

    def past_part():
        for f, value in enumerate(head(cols_one, 0, weight_one)):
            hid[0, f] = value + bias_first[...]

    load_w1.wait()

    @pl.when(ta == 0)
    def _():
        raw_halo("recv", 1)
        spread_plain(cols_one, 2, raw, 1)
        load_second.wait()
        hid_halo("start", 0)

    @pl.when(ta == 1)
    def _():
        raw_halo("recv", 0)
        spread_plain(cols_one, 0, raw, 0)
        past_part()

    mean_one, scale_one = scale_of(0, gain_first)
    raw_halo("recv", 2)
    spread_act(cols_one, 4, 2, mean_one, scale_one, shift_first)
    for f, value in enumerate(tail(cols_one, 2, weight_one)):
        hid[1, f] = value + bias_first[...]

    @pl.when(ta > 0)
    def _():
        near = time_copies(1)
        for part in (0, 1):
            near[part].wait_recv()
            column_relays("start", part)
        raw_halo("start", 1, (False,))

        def carried(which):
            spread_act(cols_one, 2, 1, mean_one, scale_one, shift_first, which)

        column_relays("recv", 0)
        column_relays("recv", 1)
        carried((1, rows))
        near[2].wait_recv()
        column_relays("start", 2)
        raw_halo("recv", 1, (False,))
        carried((0, rows + 1))
        column_relays("recv", 2)
        carried(tuple(range(2, rows)))
        if nta > 2:

            @pl.when(ta > 1)
            def _():
                for copy in time_copies(2):
                    copy.wait_recv()
                raw_halo("start", 0)
                raw_halo("recv", 0)
                spread_act(cols_one, 0, 0, mean_one, scale_one, shift_first)
                past_part()

    pair = head(cols_one, 2, weight_one)
    pair = [value + hid[1, f] for f, value in enumerate(pair)]
    flat = [value.reshape(rows * cols, chans) for value in pair]
    put_stats(1, flat[0] + flat[1], flat[0] * flat[0] + flat[1] * flat[1])
    send_stats(1)
    for f, value in enumerate(pair):
        hid[1, f] = value
    keep_edges(1, pair)
    hid_halo("start", 1)
    load_w2.wait()
    for f in range(nframe):
        total[f] = middle(raw, 2, f, slice(1, rows + 1)) + bias_second[...]

    def carried_part():
        for f, value in enumerate(head(cols_two, 0, weight_two)):
            total[f] += value

    @pl.when(ta > 0)
    def _():
        pair = tail(cols_one, 0, weight_one)
        pair = [value + hid[0, f] for f, value in enumerate(pair)]
        for f, value in enumerate(pair):
            hid[0, f] = value
        keep_edges(0, pair)
        hid_halo("start", 0)

    @pl.when(ta == 0)
    def _():
        hid_halo("recv", 0)
        spread_plain(cols_two, 0, hid_edge, 0)
        carried_part()

    mean_two, scale_two = scale_of(1, gain_second)
    hid_halo("recv", 1)
    spread_hidden(cols_two, 2, 1, mean_two, scale_two, shift_second)
    for f, value in enumerate(tail(cols_two, 0, weight_two)):
        total[f] += value

    @pl.when(ta > 0)
    def _():
        hid_halo("recv", 0)
        spread_hidden(cols_two, 0, 0, mean_two, scale_two, shift_second)
        carried_part()

    for f in range(nframe):
        out[f] = total[f].astype(out.dtype)

    for step in steps:

        @pl.when(ta + step < nta)
        def _():
            for copy in time_copies(step):
                copy.wait_send()

    raw_halo("send", 2)
    raw_halo("send", 1, (False,))

    @pl.when(ta == 0)
    def _():
        raw_halo("send", 1, (True,))

    @pl.when(ta > 0)
    def _():
        for part in range(3):
            column_relays("send", part)
        raw_halo("send", 0)

    hid_halo("send", 1)
    hid_halo("send", 0)
    for which in range(2):
        pltpu.make_async_copy(stat_in.at[which], stat_in.at[which], stat_send.at[which]).wait()


def on_device(
    sizes,
    frames,
    past_first,
    past_second,
    gain_first,
    shift_first,
    kernel_first,
    bias_first,
    gain_second,
    shift_second,
    kernel_second,
    bias_second,
):
    nframe, rows, cols, chans = frames.shape
    nha, nwa, nta = sizes
    peers = nha * nwa * nta
    line = lambda v: v
    stack = lambda k: k.reshape(3, 9 * chans, chans)
    bf16, f32 = jnp.bfloat16, jnp.float32
    hbm = pl.BlockSpec(memory_space=pltpu.HBM)
    vmem = pl.BlockSpec(memory_space=pltpu.VMEM)
    dma = pltpu.SemaphoreType.DMA
    padded = (rows + 2, cols + 2 * PAD, chans)
    sides = len(DIRECTIONS)
    return pl.pallas_call(
        functools.partial(body, sizes),
        out_shape=jax.ShapeDtypeStruct(frames.shape, bf16),
        in_specs=[hbm] * 11,
        out_specs=vmem,
        scratch_shapes=[
            pltpu.VMEM((6, 1, chans), f32),
            pltpu.VMEM((nframe, rows, cols, chans), f32),
            pltpu.VMEM((3, nframe) + padded, bf16),
            pltpu.VMEM((2, nframe) + padded, bf16),
            pltpu.VMEM((2, nframe, rows, cols, chans), f32),
            pltpu.VMEM((rows + 2, cols + PAD, chans), f32),
            pltpu.VMEM((3 * nframe, rows + 2, cols, 3 * chans), bf16),
            pltpu.VMEM((2 * nframe, rows + 2, cols, 3 * chans), bf16),
            pltpu.VMEM((3, 9 * chans, chans), bf16),
            pltpu.VMEM((3, 9 * chans, chans), bf16),
            pltpu.VMEM((2, 2, chans), f32),
            pltpu.VMEM((2, peers - 1, 2, chans), f32),
            dma((11,)),
            dma((3, sides)),
            dma((3, sides)),
            dma((2, sides)),
            dma((2, sides)),
            dma((2, 3)),
            dma((2, 3)),
            dma((3, 2)),
            dma((3, 2)),
            dma((2,)),
            dma((2,)),
        ],
        compiler_params=pltpu.CompilerParams(
            collective_id=0, has_side_effects=True, vmem_limit_bytes=62 * 1024 * 1024
        ),
        cost_estimate=pl.CostEstimate(
            flops=4 * 27 * nframe * rows * cols * chans * chans,
            bytes_accessed=4 * 1024 * 1024,
            transcendentals=4 * nframe * rows * cols * chans,
        ),
    )(
        frames,
        past_first,
        past_second,
        line(gain_first),
        line(shift_first),
        stack(kernel_first),
        line(bias_first),
        line(gain_second),
        line(shift_second),
        stack(kernel_second),
        line(bias_second),
    )


def solution(mesh):
    sizes = tuple(mesh.shape[name] for name in ("ha", "wa", "ta"))
    return jax.shard_map(
        functools.partial(on_device, sizes),
        mesh=mesh,
        in_specs=(
            P(("clips", "ta"), "ha", "wa", None),
            P("clips", "ha", "wa", None),
            P("clips", "ha", "wa", None),
        )
        + (P(),) * 8,
        out_specs=P(("clips", "ta"), "ha", "wa", None),
        check_vma=False,
    )
```

```python
import functools

import jax
import jax.numpy as jnp
from jax import lax
from jax.experimental import pallas as pl
from jax.experimental.pallas import tpu as pltpu
from jax.sharding import PartitionSpec as P

EPS = 1e-06
G = 32
PAD = 16
MESH = pl.DeviceIdType.MESH
DIRECTIONS = [(dh, dw) for dh in (-1, 0, 1) for dw in (-1, 0, 1) if (dh, dw) != (0, 0)]


def body(
    sizes,
    frames,
    past_first,
    past_second,
    gain_first_in,
    shift_first_in,
    kernel_first,
    bias_first_in,
    gain_second_in,
    shift_second_in,
    kernel_second,
    bias_second_in,
    out,
    vectors,
    total,
    raw,
    hid_edge,
    hid,
    line,
    cols_one,
    cols_two,
    weight_one,
    weight_two,
    stat_own,
    stat_in,
    local_sem,
    raw_send,
    raw_recv,
    hid_send,
    hid_recv,
    time_send,
    time_recv,
    col_send,
    col_recv,
    stat_send,
    stat_recv,
):
    nha, nwa, nta = sizes
    peers = nha * nwa * nta
    _, nframe, rows2, width, chans = raw.shape
    rows, cols = rows2 - 2, width - 2 * PAD
    ha, wa, ta = lax.axis_index("ha"), lax.axis_index("wa"), lax.axis_index("ta")
    count = float(nframe * rows * cols * (chans // G) * peers)

    def ring(at, step, size):
        return jnp.where(at + step >= size, at + step - size, at + step)

    def place(k):
        dh, dw, dt = k // (nwa * nta), k // nta % nwa, k % nta
        return {"ha": ring(ha, dh, nha), "wa": ring(wa, dw, nwa), "ta": ring(ta, dt, nta)}

    def each_peer(work):
        if peers <= 32:
            for k in range(1, peers):
                work(k)
        else:
            pl.loop(1, peers)(work)

    def inner(buf, slot):
        return buf.at[slot, :, pl.ds(1, rows), pl.ds(PAD, cols), :]

    load_frames = pltpu.make_async_copy(frames, inner(raw, 2), local_sem.at[0])
    load_past = pltpu.make_async_copy(past_first, inner(raw, jnp.maximum(1 - ta, 0)), local_sem.at[1])
    load_second = pltpu.make_async_copy(past_second, inner(hid_edge, 0), local_sem.at[2])
    vector_in = (
        gain_first_in,
        shift_first_in,
        bias_first_in,
        gain_second_in,
        shift_second_in,
        bias_second_in,
    )
    load_vectors = [
        pltpu.make_async_copy(ref, vectors.at[i, 0], local_sem.at[5 + i])
        for i, ref in enumerate(vector_in)
    ]
    gain_first, shift_first, bias_first, gain_second, shift_second, bias_second = (
        vectors.at[i] for i in range(6)
    )
    load_w1 = pltpu.make_async_copy(kernel_first, weight_one, local_sem.at[3])
    load_w2 = pltpu.make_async_copy(kernel_second, weight_two, local_sem.at[4])

    def halo_copy(buf, slot, send, recv, d):
        dh, dw = DIRECTIONS[d]
        row_from, row_to, nrow = {-1: (1, rows + 1, 1), 0: (1, 1, rows), 1: (rows, 0, 1)}[dh]
        col_from, col_to, ncol = {
            -1: (PAD, PAD + cols, PAD),
            0: (PAD, PAD, cols),
            1: (cols, 0, PAD),
        }[dw]
        copy = pltpu.make_async_remote_copy(
            src_ref=buf.at[slot, :, pl.ds(row_from, nrow), pl.ds(col_from, ncol), :],
            dst_ref=buf.at[slot, :, pl.ds(row_to, nrow), pl.ds(col_to, ncol), :],
            send_sem=send.at[slot, d],
            recv_sem=recv.at[slot, d],
            device_id={"ha": ha + dh, "wa": wa + dw},
            device_id_type=MESH,
        )
        to_h, to_w = ha + dh, wa + dw
        from_h, from_w = ha - dh, wa - dw
        goes = (to_h >= 0) & (to_h < nha) & (to_w >= 0) & (to_w < nwa)
        comes = (from_h >= 0) & (from_h < nha) & (from_w >= 0) & (from_w < nwa)
        return copy, goes, comes

    def halo(action, buf, slot, send, recv, beside):
        for d in range(len(DIRECTIONS)):
            if (DIRECTIONS[d][0] == 0) not in beside:
                continue
            copy, goes, comes = halo_copy(buf, slot, send, recv, d)
            if action == "start":
                pl.when(goes)(copy.start)
            elif action == "recv":
                pl.when(comes)(copy.wait_recv)
            else:
                pl.when(goes)(copy.wait_send)

    def raw_halo(action, slot, beside=(False, True)):
        halo(action, raw, slot, raw_send, raw_recv, beside)

    def hid_halo(action, slot):
        halo(action, hid_edge, slot, hid_send, hid_recv, (False, True))

    row_parts = ((1, 1), (rows, 1), (2, rows - 2))

    def time_copies(step):
        slot = 2 - step
        return [
            pltpu.make_async_remote_copy(
                src_ref=raw.at[2, :, pl.ds(first, n), pl.ds(PAD, cols), :],
                dst_ref=raw.at[slot, :, pl.ds(first, n), pl.ds(PAD, cols), :],
                send_sem=time_send.at[step - 1, i],
                recv_sem=time_recv.at[step - 1, i],
                device_id={"ta": ta + step},
                device_id_type=MESH,
            )
            for i, (first, n) in enumerate(row_parts)
        ]

    def column_relays(action, part):
        first, n = row_parts[part]
        for side, dw in enumerate((-1, 1)):
            col_from, col_to = (PAD, PAD + cols) if dw < 0 else (cols, 0)
            copy = pltpu.make_async_remote_copy(
                src_ref=raw.at[1, :, pl.ds(first, n), pl.ds(col_from, PAD), :],
                dst_ref=raw.at[1, :, pl.ds(first, n), pl.ds(col_to, PAD), :],
                send_sem=col_send.at[part, side],
                recv_sem=col_recv.at[part, side],
                device_id={"wa": wa + dw},
                device_id_type=MESH,
            )
            goes = (wa + dw >= 0) & (wa + dw < nwa)
            comes = (wa - dw >= 0) & (wa - dw < nwa)
            if action == "start":
                pl.when(goes)(copy.start)
            elif action == "recv":
                pl.when(comes)(copy.wait_recv)
            else:
                pl.when(goes)(copy.wait_send)

    steps = [step for step in (1, 2) if step < nta]

    def stat_copy(which, k):
        return pltpu.make_async_remote_copy(
            src_ref=stat_own.at[which],
            dst_ref=stat_in.at[which, k - 1],
            send_sem=stat_send.at[which],
            recv_sem=stat_recv.at[which],
            device_id=place(k),
            device_id_type=MESH,
        )

    def send_stats(which):
        each_peer(lambda k: stat_copy(which, k).start())

    def group_total(which):
        pltpu.make_async_copy(stat_in.at[which], stat_in.at[which], stat_recv.at[which]).wait()
        sums = stat_own[which] + jnp.sum(stat_in[which], axis=0)
        lane = lax.broadcasted_iota(jnp.int32, sums.shape, 1)
        for shift in (1, 2):
            low = lax.rem(lane, 2 * shift) < shift
            sums = sums + jnp.where(
                low, pltpu.roll(sums, chans - shift, 1), pltpu.roll(sums, shift, 1)
            )
        return sums

    def scale_of(which, gain):
        sums = group_total(which)
        mean = sums[0:1] / count
        inverse = lax.rsqrt(sums[1:2] / count - mean * mean + EPS)
        return mean, inverse * gain[...]

    def put_stats(which, first, second):
        stat_own[which, 0:1, :] = jnp.sum(first, axis=0, keepdims=True)
        stat_own[which, 1:2, :] = jnp.sum(second, axis=0, keepdims=True)

    def act(value, mean, scale, shift):
        half = (value - mean) * (0.5 * scale) + 0.5 * shift[...]
        return half + half * jnp.tanh(half)

    half_pad = PAD // 2

    def spread(dst, frame, row, left, mid, right):
        left = jnp.where(wa > 0, left, 0.0)
        right = jnp.where(wa < nwa - 1, right, 0.0)
        if row in (0, rows + 1):
            live = (ha > 0) if row == 0 else (ha < nha - 1)
            left, mid, right = (jnp.where(live, value, 0.0) for value in (left, mid, right))
        line[row, 0:half_pad] = left
        line[row, half_pad : half_pad + cols] = mid
        line[row, half_pad + cols : PAD + cols] = right
        before = line[row, half_pad - 1 : half_pad - 1 + cols]
        after = line[row, half_pad + 1 : half_pad + 1 + cols]
        dst[frame, row, :, 0:chans] = before.astype(jnp.bfloat16)
        dst[frame, row, :, chans : 2 * chans] = mid.astype(jnp.bfloat16)
        dst[frame, row, :, 2 * chans :] = after.astype(jnp.bfloat16)

    def edges(buf, slot, f, r):
        left = buf[slot, f, r, 0:PAD].astype(jnp.float32)[half_pad:]
        right = buf[slot, f, r, PAD + cols :].astype(jnp.float32)[:half_pad]
        return left, right

    def middle(buf, slot, f, r):
        return buf[slot, f, r, PAD : PAD + cols].astype(jnp.float32)

    def spread_frames(dst, base, buf, slot, change, own=None, which=None):
        @pl.loop(0, nframe)
        def _(f):
            for r in which or range(rows2):
                left, right = edges(buf, slot, f, r)
                if own is not None and 0 < r < rows + 1:
                    mid = own[slot, f, r - 1]
                else:
                    mid = middle(buf, slot, f, r)
                spread(dst, base + f, r, change(left), change(mid), change(right))

    def spread_plain(dst, base, buf, slot):
        spread_frames(dst, base, buf, slot, lambda value: value)

    def spread_act(dst, base, slot, mean, scale, shift, which=None):
        spread_frames(
            dst, base, raw, slot, lambda value: act(value, mean, scale, shift), None, which
        )

    def spread_hidden(dst, base, slot, mean, scale, shift):
        spread_frames(
            dst, base, hid_edge, slot, lambda value: act(value, mean, scale, shift), hid
        )

    def slab(src, f):
        return jnp.concatenate(
            [src[f, b : b + rows].reshape(rows * cols, 3 * chans) for b in range(3)], axis=1
        )

    def dot(left, right):
        return jnp.dot(left, right, preferred_element_type=jnp.float32)

    def shaped(*pair):
        return [value.reshape(rows, cols, chans) for value in pair]

    def head(src, base, weight):
        both = dot(slab(src, base + 1), jnp.concatenate([weight[1], weight[0]], axis=1))
        one = both[:, :chans] + dot(slab(src, base), weight[0])
        return shaped(one, both[:, chans:])

    def tail(src, base, weight):
        both = dot(slab(src, base + 2), jnp.concatenate([weight[2], weight[1]], axis=1))
        two = both[:, chans:] + dot(slab(src, base + 3), weight[2])
        return shaped(both[:, :chans], two)

    def keep_edges(slot, pair):
        for f, value in enumerate(pair):
            hid_edge[slot, f, 1 : rows + 1, PAD : PAD + cols, :] = value.astype(jnp.bfloat16)

    load_frames.start()

    @pl.when(ta < 2)
    def _():
        load_past.start()

    @pl.when(ta == 0)
    def _():
        load_second.start()

    barrier = pltpu.get_barrier_semaphore()

    each_peer(
        lambda k: pl.semaphore_signal(barrier, inc=1, device_id=place(k), device_id_type=MESH)
    )

    for copy in load_vectors:
        copy.start()
    load_w1.start()
    load_w2.start()
    load_frames.wait()
    first = jnp.zeros((cols, chans), jnp.float32)
    second = jnp.zeros((cols, chans), jnp.float32)
    for f in range(nframe):
        for r in range(rows):
            value = raw[2, f, 1 + r, PAD : PAD + cols, :].astype(jnp.float32)
            first = first + value
            second = second + value * value
    put_stats(0, first, second)
    for copy in load_vectors:
        copy.wait()
    pl.semaphore_wait(barrier, peers - 1)
    send_stats(0)

    for step in steps:

        @pl.when(ta + step < nta)
        def _():
            for copy in time_copies(step):
                copy.start()

    raw_halo("start", 2)

    @pl.when(ta == 0)
    def _():
        load_past.wait()
        raw_halo("start", 1)

    @pl.when(ta == 1)
    def _():
        load_past.wait()
        raw_halo("start", 0)

    mean_one, scale_one = scale_of(0, gain_first)
    raw_halo("recv", 2)
    spread_act(cols_one, 4, 2, mean_one, scale_one, shift_first)
    load_w1.wait()
    for f, value in enumerate(tail(cols_one, 2, weight_one)):
        hid[1, f] = value + bias_first[...]

    @pl.when(ta == 0)
    def _():
        load_second.wait()
        hid_halo("start", 0)
        raw_halo("recv", 1)
        spread_plain(cols_one, 2, raw, 1)

    def past_part():
        for f, value in enumerate(head(cols_one, 0, weight_one)):
            hid[0, f] = value + bias_first[...]

    @pl.when(ta > 0)
    def _():
        @pl.when(ta == 1)
        def _():
            raw_halo("recv", 0)
            spread_plain(cols_one, 0, raw, 0)

        near = time_copies(1)
        for part in (0, 1):
            near[part].wait_recv()
            column_relays("start", part)
        raw_halo("start", 1, (False,))

        @pl.when(ta == 1)
        def _():
            past_part()

        def carried(which):
            spread_act(cols_one, 2, 1, mean_one, scale_one, shift_first, which)

        column_relays("recv", 0)
        column_relays("recv", 1)
        carried((1, rows))
        near[2].wait_recv()
        column_relays("start", 2)
        raw_halo("recv", 1, (False,))
        carried((0, rows + 1))
        column_relays("recv", 2)
        carried(tuple(range(2, rows)))
        if nta > 2:

            @pl.when(ta > 1)
            def _():
                for copy in time_copies(2):
                    copy.wait_recv()
                raw_halo("start", 0)
                raw_halo("recv", 0)
                spread_act(cols_one, 0, 0, mean_one, scale_one, shift_first)
                past_part()

    pair = head(cols_one, 2, weight_one)
    pair = [value + hid[1, f] for f, value in enumerate(pair)]
    flat = [value.reshape(rows * cols, chans) for value in pair]
    put_stats(1, flat[0] + flat[1], flat[0] * flat[0] + flat[1] * flat[1])
    send_stats(1)
    for f, value in enumerate(pair):
        hid[1, f] = value
    keep_edges(1, pair)
    hid_halo("start", 1)
    load_w2.wait()
    for f in range(nframe):
        total[f] = middle(raw, 2, f, slice(1, rows + 1)) + bias_second[...]

    def carried_part():
        for f, value in enumerate(head(cols_two, 0, weight_two)):
            total[f] += value

    @pl.when(ta > 0)
    def _():
        pair = tail(cols_one, 0, weight_one)
        pair = [value + hid[0, f] for f, value in enumerate(pair)]
        for f, value in enumerate(pair):
            hid[0, f] = value
        keep_edges(0, pair)
        hid_halo("start", 0)

    @pl.when(ta == 0)
    def _():
        hid_halo("recv", 0)
        spread_plain(cols_two, 0, hid_edge, 0)
        carried_part()

    mean_two, scale_two = scale_of(1, gain_second)
    hid_halo("recv", 1)
    spread_hidden(cols_two, 2, 1, mean_two, scale_two, shift_second)
    for f, value in enumerate(tail(cols_two, 0, weight_two)):
        total[f] += value

    @pl.when(ta > 0)
    def _():
        hid_halo("recv", 0)
        spread_hidden(cols_two, 0, 0, mean_two, scale_two, shift_second)
        carried_part()

    for f in range(nframe):
        out[f] = total[f].astype(out.dtype)

    for step in steps:

        @pl.when(ta + step < nta)
        def _():
            for copy in time_copies(step):
                copy.wait_send()

    raw_halo("send", 2)
    raw_halo("send", 1, (False,))

    @pl.when(ta == 0)
    def _():
        raw_halo("send", 1, (True,))

    @pl.when(ta > 0)
    def _():
        for part in range(3):
            column_relays("send", part)
        raw_halo("send", 0)

    hid_halo("send", 1)
    hid_halo("send", 0)
    for which in range(2):
        pltpu.make_async_copy(stat_in.at[which], stat_in.at[which], stat_send.at[which]).wait()


def on_device(
    sizes,
    frames,
    past_first,
    past_second,
    gain_first,
    shift_first,
    kernel_first,
    bias_first,
    gain_second,
    shift_second,
    kernel_second,
    bias_second,
):
    nframe, rows, cols, chans = frames.shape
    nha, nwa, nta = sizes
    peers = nha * nwa * nta
    line = lambda v: v
    stack = lambda k: k.reshape(3, 9 * chans, chans)
    bf16, f32 = jnp.bfloat16, jnp.float32
    hbm = pl.BlockSpec(memory_space=pltpu.HBM)
    vmem = pl.BlockSpec(memory_space=pltpu.VMEM)
    dma = pltpu.SemaphoreType.DMA
    padded = (rows + 2, cols + 2 * PAD, chans)
    sides = len(DIRECTIONS)
    return pl.pallas_call(
        functools.partial(body, sizes),
        out_shape=jax.ShapeDtypeStruct(frames.shape, bf16),
        in_specs=[hbm] * 11,
        out_specs=vmem,
        scratch_shapes=[
            pltpu.VMEM((6, 1, chans), f32),
            pltpu.VMEM((nframe, rows, cols, chans), f32),
            pltpu.VMEM((3, nframe) + padded, bf16),
            pltpu.VMEM((2, nframe) + padded, bf16),
            pltpu.VMEM((2, nframe, rows, cols, chans), f32),
            pltpu.VMEM((rows + 2, cols + PAD, chans), f32),
            pltpu.VMEM((3 * nframe, rows + 2, cols, 3 * chans), bf16),
            pltpu.VMEM((2 * nframe, rows + 2, cols, 3 * chans), bf16),
            pltpu.VMEM((3, 9 * chans, chans), bf16),
            pltpu.VMEM((3, 9 * chans, chans), bf16),
            pltpu.VMEM((2, 2, chans), f32),
            pltpu.VMEM((2, peers - 1, 2, chans), f32),
            dma((11,)),
            dma((3, sides)),
            dma((3, sides)),
            dma((2, sides)),
            dma((2, sides)),
            dma((2, 3)),
            dma((2, 3)),
            dma((3, 2)),
            dma((3, 2)),
            dma((2,)),
            dma((2,)),
        ],
        compiler_params=pltpu.CompilerParams(
            collective_id=0, has_side_effects=True, vmem_limit_bytes=62 * 1024 * 1024
        ),
        cost_estimate=pl.CostEstimate(
            flops=4 * 27 * nframe * rows * cols * chans * chans,
            bytes_accessed=4 * 1024 * 1024,
            transcendentals=4 * nframe * rows * cols * chans,
        ),
    )(
        frames,
        past_first,
        past_second,
        line(gain_first),
        line(shift_first),
        stack(kernel_first),
        line(bias_first),
        line(gain_second),
        line(shift_second),
        stack(kernel_second),
        line(bias_second),
    )


def solution(mesh):
    sizes = tuple(mesh.shape[name] for name in ("ha", "wa", "ta"))
    return jax.shard_map(
        functools.partial(on_device, sizes),
        mesh=mesh,
        in_specs=(
            P(("clips", "ta"), "ha", "wa", None),
            P("clips", "ha", "wa", None),
            P("clips", "ha", "wa", None),
        )
        + (P(),) * 8,
        out_specs=P(("clips", "ta"), "ha", "wa", None),
        check_vma=False,
    )
```
